32 devices in a mesh: ao: 8 (over z, x), ri: 4 (over y, core).
Axes of the slice: x: 2, y: 2, z: 4, core: 2. Of those that a mesh axis runs over, the one named last changes fastest.
Arguments:
- three_center: bfloat16 [64, 3072, 128], P('ri', 'ao'), may hold values from -0.19921875 to 0.19921875
- occ_band: bfloat16 [1024, 640], P('ao'), may hold values from -0.3125 to 0.3125
- virt_band: bfloat16 [1024, 384], P('ao'), may hold values from -0.3125 to 0.3125
- three_mask: int32 [8, 3], P('ao'), may hold values 0 or 1
- occ_mask: int32 [8, 5], P('ao'), may hold values 0 or 1
- virt_mask: int32 [8, 3], P('ao'), may hold values 0 or 1
Outputs:
- chi: float32 [64, 64], P('ri')
The draws below stay inside these ranges and needn't reach their ends.
All inputs are finite; a program needn't handle non-finite values. No bound on the sum of `three_mask` or of `occ_mask` or of `virt_mask` on one device may be relied on, other than what follows from the above.
Results may differ from the reference program's by a relative error of at most 0.004.
Values may be sent and summed in bfloat16 or wider, within the bound.
No kernel may reach another device: no remote copies, remote signals or barrier semaphores. Data moves between devices by JAX's collectives and lax.ppermute only.
A program may use at most 64 MiB of HBM per device.

```python
import jax
import jax.numpy as jnp
from jax import lax

TILE = 128
PT = 64
NT = 8


def plant(result, key, smallest, high):
    dims = result.shape
    spot = [jax.random.randint(jax.random.fold_in(key, axis), (), 0, dims[axis]) for axis in range(len(dims))]
    result = result.at[tuple(spot)].set(smallest)
    longest = dims.index(max(dims))
    spot[longest] = (spot[longest] + 1) % dims[longest]
    return result.at[tuple(spot)].set(high)


def steps_of(rng, dims, cuts, low, largest):
    loudness, own = 1.0, jax.random.fold_in(rng, 6)
    for axis_at, blocks in cuts:
        draws = jnp.exp(jax.random.uniform(jax.random.fold_in(own, axis_at), (blocks,), jnp.float32, low / len(cuts), largest / len(cuts)))
        loudness = loudness * jnp.repeat(draws, dims[axis_at] // blocks).reshape([-1 if axis == axis_at else 1 for axis in range(len(dims))])
    return loudness


def normal_values(own_key, shape, scale, limit, split=(), kind=jnp.bfloat16):
    level = steps_of(own_key, shape, split, -0.22, 0.18) if split else 1.0
    drawn = jax.random.normal(own_key, shape, jnp.float32) * scale * level
    return jnp.minimum(jnp.maximum(drawn, -limit), limit).astype(kind)


def setup_inputs(seed: int = 0) -> dict:
    keys = jax.random.split(jax.random.key(seed), 7)
    three_center = normal_values(keys[0], (PT, NT * 3 * TILE, TILE), 0.03, 0.19921875, ((0, 4), (1, 8)))
    occ_band = normal_values(keys[1], (NT * TILE, 5 * TILE), (3 * TILE) ** -0.5, 0.3125, ((0, 8),))
    virt_band = normal_values(keys[2], (NT * TILE, 3 * TILE), (3 * TILE) ** -0.5, 0.3125, ((0, 8),))
    three_mask = plant((jax.random.randint(keys[3], (NT, 3), 0, 4) < 3).astype(jnp.int32), jax.random.fold_in(keys[3], 1), 0, 1)
    occ_mask = plant((jax.random.randint(keys[4], (NT, 5), 0, 4) < 3).astype(jnp.int32), jax.random.fold_in(keys[4], 1), 0, 1)
    virt_mask = plant((jax.random.randint(keys[5], (NT, 3), 0, 4) < 3).astype(jnp.int32), jax.random.fold_in(keys[5], 1), 0, 1)
    return dict(three_center=three_center, occ_band=occ_band, virt_band=virt_band, three_mask=three_mask, occ_mask=occ_mask, virt_mask=virt_mask)


def reference(three_center, occ_band, virt_band, three_mask, occ_mask, virt_mask):
    tile_size = TILE
    tiles = NT
    batch = three_center.shape[0]
    live_b = three_center.reshape(batch, tiles, 3, tile_size, tile_size) * three_mask.astype(three_center.dtype)[None, :, :, None, None]
    live_occ = (occ_band.reshape(tiles, tile_size, 5, tile_size) * occ_mask.astype(occ_band.dtype)[:, None, :, None]).reshape(tiles, tile_size, 5 * tile_size)
    live_virt = (virt_band.reshape(tiles, tile_size, 3, tile_size) * virt_mask.astype(virt_band.dtype)[:, None, :, None]).reshape(tiles, tile_size, 3 * tile_size)
    blank = jnp.zeros((tile_size, tile_size), occ_band.dtype)

    def build_m(index):
        first = jnp.take(live_occ, ((index - 1) % tiles).astype(jnp.int32), axis=0)
        middle = jnp.take(live_occ, index.astype(jnp.int32), axis=0)
        last = jnp.take(live_occ, ((index + 1) % tiles).astype(jnp.int32), axis=0)
        green_block = jnp.concatenate([
            jnp.concatenate([first[:, tile_size:], blank], 1),
            middle,
            jnp.concatenate([blank, last[:, :4 * tile_size]], 1)], 0)
        own_b = jnp.take(live_b, index.astype(jnp.int32), axis=1).reshape(batch, 3 * tile_size, tile_size)
        contracted = jnp.einsum("ml,pmn->pln", green_block.astype(jnp.float32), own_b.astype(jnp.float32))
        return contracted.astype(jnp.bfloat16)

    indices = jnp.arange(tiles, dtype=jnp.int32)
    m_all = lax.map(build_m, indices)

    def add_chi(total, index):
        left = jnp.take(m_all, ((index - 1) % tiles).astype(jnp.int32), axis=0)[:, 2 * tile_size:5 * tile_size]
        own = jnp.take(m_all, index.astype(jnp.int32), axis=0)[:, tile_size:4 * tile_size]
        right = jnp.take(m_all, ((index + 1) % tiles).astype(jnp.int32), axis=0)[:, 0:3 * tile_size]
        needed = jnp.concatenate([left, own, right], 2)
        virt_rows = jnp.take(live_virt, index.astype(jnp.int32), axis=0)
        product = jnp.einsum("plv,sv->pls", needed.astype(jnp.float32), virt_rows.astype(jnp.float32)).astype(jnp.bfloat16)
        own_b = jnp.take(live_b, index.astype(jnp.int32), axis=1).reshape(batch, -1)
        part = jnp.dot(product.reshape(batch, -1), own_b.T, preferred_element_type=jnp.float32)
        return total + part, None

    total, _ = lax.scan(add_chi, jnp.zeros((batch, batch), jnp.float32), indices)
    return -total
```

```python
import functools

import jax
import jax.numpy as jnp
from jax import lax
from jax.experimental import pallas as pl
from jax.experimental.pallas import tpu as pltpu
from jax.sharding import PartitionSpec as P

F32, BF16 = jnp.float32, jnp.bfloat16
VMEM_LIMIT = 56 * 1024 * 1024
PARAMS = pltpu.CompilerParams(vmem_limit_bytes=VMEM_LIMIT)
ANY = pl.BlockSpec(memory_space=pl.ANY)
VMEM = pl.BlockSpec(memory_space=pltpu.VMEM)
SMEM = pl.BlockSpec(memory_space=pltpu.SMEM)
BOTH = ("ao", "ri")
LARGE = pl.CostEstimate(flops=10**11, bytes_accessed=10**9, transcendentals=0)
LITTLE = pl.CostEstimate(flops=1024, bytes_accessed=1024, transcendentals=0)


def call(kernel, name, out_shape, in_specs, out_specs=VMEM, **more):
    return pl.pallas_call(
        kernel,
        name=name,
        out_shape=out_shape,
        in_specs=in_specs,
        out_specs=out_specs,
        compiler_params=PARAMS,
        cost_estimate=LARGE if name in ("halo_panels", "own_m") else LITTLE,
        **more,
    )


def shape(*dims, dtype=BF16):
    return jax.ShapeDtypeStruct(dims, dtype)


def dot_nn(a, b, **more):
    return lax.dot_general(a, b, (((1,), (0,)), ((), ())), preferred_element_type=F32, **more)


def dot_nt(a, b):
    return lax.dot_general(a, b, (((1,), (1,)), ((), ())), preferred_element_type=F32)


def when_core(core, even, odd):
    pl.when(core == 0)(even)
    pl.when(core != 0)(odd)


def pack_kernel(
    core_ref, occ_mask, virt_mask, three_mask, occ_ref, virt_ref, src_ref,
    one_ref, two_ref, near_ref, late_ref, sems,
):
    tile, half = occ_ref.shape[0], near_ref.shape[0]
    moves = [
        pltpu.make_async_copy(src_ref.at[:half], near_ref, sems.at[0]),
        pltpu.make_async_copy(src_ref.at[half:], late_ref, sems.at[1]),
    ]
    for move in moves:
        move.start()

    def occ(k):
        return occ_ref[:, k * tile : (k + 1) * tile] * occ_mask[0, k].astype(BF16)

    def even():
        for k in range(4):
            one_ref[:tile, k * tile : (k + 1) * tile] = occ(k)
        one_ref[:tile, 4 * tile :] = virt_ref[:, :tile] * virt_mask[0, 0].astype(BF16)

    def odd():
        for k in range(3):
            one_ref[:tile, k * tile : (k + 1) * tile] = occ(k + 2)
        one_ref[:tile, 3 * tile :] = jnp.zeros((tile, 2 * tile), BF16)

    when_core(core_ref[0], even, odd)
    one_ref[tile:, :] = jnp.zeros((16, 5 * tile), BF16)
    for k in range(3):
        flag = jnp.full((16, tile), three_mask[0, k].astype(F32), F32)
        one_ref[tile:, k * tile : (k + 1) * tile] = flag.astype(BF16)
    for k in range(2):
        two_ref[:, k * tile : (k + 1) * tile] = occ(k)
    for move in moves:
        move.wait()


def tables_kernel(
    core_ref, occ_mask, virt_mask, three_mask, occ_ref, virt_ref, one_ref, two_ref, far_ref, after_ref,
    own_ref, halo_ref, virt_own_ref, virt_next_ref, lower, upper,
):
    tile = occ_ref.shape[0]

    def even():
        lower[...], upper[...] = far_ref[...], one_ref[...]

    def odd():
        lower[...], upper[...] = one_ref[...], far_ref[...]

    when_core(core_ref[0], even, odd)

    def cols(k):
        return slice(k * tile, (k + 1) * tile)

    def entry(mu, lam):
        if abs(mu - lam) > 2:
            return None
        if mu == -1:
            return lower[:tile, cols(lam + 1)]
        if mu == 0:
            return occ_ref[:, cols(lam + 2)] * occ_mask[0, lam + 2].astype(BF16)
        if mu == 1:
            return upper[:tile, cols(lam + 1)]
        return two_ref[:, cols(lam)]

    blank = jnp.zeros((tile, tile), BF16)
    own = [three_mask[0, k].astype(BF16) for k in range(3)]
    after = [upper[tile : tile + 1, cols(k)] for k in range(3)]
    for lam in range(-1, 2):
        for mu in range(-1, 3):
            block = entry(mu, lam)
            if block is not None:
                block = block.T * own[lam + 1]
            if mu < 2:
                own_ref[cols(lam + 1), cols(mu + 1)] = block * own[mu + 1]
            if mu > -1:
                halo_ref[cols(lam + 1), cols(mu)] = blank if block is None else block * after[mu]
    for mu in range(-1, 2):
        for lam in range(3):
            block = entry(mu, lam)
            value = blank if block is None else block * own[mu + 1] * after[lam]
            halo_ref[cols(mu + 4), cols(lam)] = value
    for k in range(2):
        virt_own_ref[:, cols(k)] = virt_ref[:, cols(k + 1)] * virt_mask[0, k + 1].astype(BF16)
    virt_next_ref[...] = upper[:tile, 4 * tile :]


def relayout_kernel(after_ref, src_ref, out_ref):
    out_ref[...] = jnp.swapaxes(src_ref[...], 0, 1)


def relayout(after, src, steps=3):
    batch, height, width = src.shape
    part = height // steps
    return call(
        relayout_kernel, "relayout", shape(height, batch, width),
        [ANY, pl.BlockSpec((batch, part, width), lambda i: (0, i, 0))],
        pl.BlockSpec((part, batch, width), lambda i: (i, 0, 0)),
        grid=(steps,),
    )(after, src)


def far_kernel(after_ref, near_ref, other_ref, out_ref, held, sems):
    batch, height, width = held.shape[1:]
    moves = [
        pltpu.make_async_copy(ref, held.at[k], sems.at[k])
        for k, ref in enumerate((near_ref, other_ref))
    ]
    for move in moves:
        move.start()
    for move in moves:
        move.wait()
    out_ref[...] = jnp.swapaxes(held[...].reshape(2 * batch, height, width), 0, 1)


def far_rows(after, near, other):
    batch, height, width = near.shape
    return call(
        far_kernel, "far_rows", shape(height, 2 * batch, width), [ANY] * 3,
        scratch_shapes=[
            pltpu.VMEM((2, batch, height, width), BF16),
            pltpu.SemaphoreType.DMA((2,)),
        ],
    )(after, near, other)


def own_m_kernel(green_ref, src_ref, *rest):
    outs, wide = rest[:2], rest[2]
    batch, _, width = src_ref.shape
    height, half = green_ref.shape[0], batch // 2
    for k, out_ref in enumerate(outs):
        for p in range(0, half, 2):
            pair = jnp.concatenate([src_ref[k * half + p], src_ref[k * half + p + 1]], 1)
            both = dot_nn(green_ref[...], pair)
            wide[k, pl.ds(p, height, half), :] = both[:, :width]
            wide[k, pl.ds(p + 1, height, half), :] = both[:, width:]
        out_ref[...] = wide[k].astype(BF16)


def own_m(green, src):
    batch, height, width = src.shape
    rows = width * batch // 2
    return call(
        own_m_kernel, "own_m", [shape(height * batch // 2, width)] * 2,
        [
            pl.BlockSpec((width, height), lambda i: (i, 0)),
            pl.BlockSpec((batch, height, width), lambda i: (0, 0, 0)),
        ],
        [pl.BlockSpec((rows, width), lambda i: (i, 0))] * 2,
        grid=(height // width,),
        scratch_shapes=[pltpu.VMEM((2, rows, width), F32)],
    )(green, src)


def halo_kernel(
    after_ref, halo_ref, m_ref, green_ref, virt_own_ref, virt_next_ref, out_ref,
    held, m_own, wide_m, wide_u, sems,
):
    batch, height, width = held.shape
    halo_move = pltpu.make_async_copy(halo_ref, held, sems.at[0])
    halo_move.start()
    m_move = pltpu.make_async_copy(m_ref, m_own, sems.at[1])
    m_move.start()
    halo_move.wait()
    for p in range(0, batch, 2):
        pair = jnp.concatenate([held[p], held[p + 1]], 1)
        both = dot_nn(green_ref[...], pair)
        wide_m[pl.ds(p, height, batch), :] = both[:height, :width]
        wide_m[pl.ds(p + 1, height, batch), :] = both[:height, width:]
        wide_u[pl.ds(p, height, batch), :] = both[height:, :width]
        wide_u[pl.ds(p + 1, height, batch), :] = both[height:, width:]
    m_move.wait()
    group = height // 6

    def second_stage(step, carry):
        at = pl.multiple_of(step * group, group)
        rows = pl.ds(pl.multiple_of(at * batch, group * batch), group * batch)
        both = jnp.concatenate([m_own[rows, :], wide_m[rows, :].astype(BF16)], 1)
        x = dot_nt(both, virt_own_ref[...]).reshape(group, batch, width)
        v = dot_nn(wide_u[rows, :].astype(BF16), virt_next_ref[...]).reshape(group, batch, width)
        out_ref[pl.ds(at, group)] = jnp.concatenate([x, v], 1).astype(BF16)
        return carry

    lax.fori_loop(0, height // group, second_stage, 0)


def halo_panels(after, halo, m_own, green, virt_own, virt_next):
    batch, height, width = halo.shape
    return call(
        halo_kernel, "halo_panels", shape(height, 2 * batch, width),
        [ANY] * 3 + [VMEM] * 3,
        scratch_shapes=[
            pltpu.VMEM((batch, height, width), BF16),
            pltpu.VMEM((height * batch, width), BF16),
            pltpu.VMEM((height * batch, width), F32),
            pltpu.VMEM((height * batch, width), F32),
            pltpu.SemaphoreType.DMA((2,)),
        ],
    )(after, halo, m_own, green, virt_own, virt_next)


def contract_kernel(lefts, rights, group, place_ref, *refs):
    out_ref, total_ref = refs[-2:]
    left, right = refs[:lefts], refs[lefts : lefts + rights]
    step, steps = pl.program_id(0), pl.num_programs(0)

    @pl.when(step == 0)
    def _():
        total_ref[...] = jnp.zeros_like(total_ref)

    total = None
    for at in range(0, left[0].shape[0], group):
        sides = [
            jnp.concatenate(
                [jnp.concatenate([ref[at + k] for k in range(group)], 1) for ref in side], 0
            )
            for side in (left, right)
        ]
        part = dot_nt(*sides)
        total = part if total is None else total + part
    total_ref[...] += total

    @pl.when(step == steps - 1)
    def _():
        lines, chunks, deep, wide = out_ref.shape
        rows, cols = total_ref.shape
        batch = rows // 2
        half = batch // 2
        exact = dict(precision=lax.Precision.HIGHEST)
        source = lax.broadcasted_iota(jnp.int32, (cols, cols), 0)
        target = lax.broadcasted_iota(jnp.int32, (cols, cols), 1)
        block, within = source // batch, source % batch
        near = cols - 2 * batch
        place = jnp.zeros((cols, cols), jnp.int32)
        for k in range(cols // batch - 2):
            place = jnp.where(block == k, place_ref[k] * batch + within, place)
        for k in range(2):
            for j in range(2):
                low = near + k * batch + j * half
                mine = (source >= low) & (source < low + half)
                place = jnp.where(
                    mine, place_ref[cols // batch - 2 + j] * batch + k * half + source - low, place
                )
        spread = jnp.where(place == target, 1.0, 0.0).astype(F32)
        placed = dot_nn(total_ref[...], spread, **exact)

        row = lax.broadcasted_iota(jnp.int32, (cols, rows), 0) - place_ref[0] * batch
        have = lax.broadcasted_iota(jnp.int32, (cols, rows), 1)
        chunk, part, index = have // batch, have % batch // half, have % half
        at = (row == chunk * half + index) & (row >= 0) & (row < batch)
        pick_x = jnp.where(at & (part == 0), 1.0, 0.0).astype(F32)
        pick_v = jnp.where(at & (part == 1), 1.0, 0.0).astype(F32)
        result = dot_nn(pick_x, placed, **exact) + dot_nn(pick_v, placed, **exact).T
        fold = batch // deep
        for k in range(chunks):
            piece = jnp.concatenate(
                [result[k * batch + j * deep : k * batch + (j + 1) * deep] for j in range(fold)], 1
            )
            for line in range(lines):
                out_ref[line, k] = piece


def contract(places, lefts, rights, lines, steps=3):
    height, _, width = lefts[0].shape
    part = height // steps
    rows, cols = [sum(a.shape[1] for a in side) for side in (lefts, rights)]
    batch = rows // 2
    fold = max(1, width // cols)
    dims = (lines, cols // batch, batch // fold, cols * fold)
    return call(
        functools.partial(contract_kernel, len(lefts), len(rights), 16), "contract",
        shape(*dims, dtype=F32),
        [SMEM] + [pl.BlockSpec((part, a.shape[1], width), lambda i: (i, 0, 0)) for a in lefts + rights],
        pl.BlockSpec(dims, lambda i: (0, 0, 0, 0)),
        grid=(steps,),
        scratch_shapes=[pltpu.VMEM((rows, cols), F32)],
    )(places, *lefts, *rights)


def total_kernel(src_ref, out_ref):
    total = -jnp.sum(src_ref[...], 0)
    deep, cols = total.shape[0], out_ref.shape[1]
    for j in range(out_ref.shape[0] // deep):
        out_ref[j * deep : (j + 1) * deep, :] = total[:, j * cols : (j + 1) * cols]


def shifted(value, axis, distance):
    size = lax.axis_size(axis)
    return lax.ppermute(value, axis, [(i, (i + distance) % size) for i in range(size)])


def per_device(three_center, occ_band, virt_band, three_mask, occ_mask, virt_mask):
    batch, height, tile = three_center.shape
    lines, groups = lax.axis_size("ao"), lax.axis_size("ri")
    mine = lax.axis_index("ri")
    core = (mine % 2).astype(jnp.int32)[None]
    half = batch // 2

    def mixed(near, far):
        pairs = []
        for a in range(lines):
            for r in range(groups):
                da, dr = near if r % 2 else far
                pairs.append((a * groups + r, ((a + da) % lines) * groups + (r + dr) % groups))
        return pairs

    def partner(value):
        return lax.ppermute(value, "ri", [(i, i ^ 1) for i in range(groups)])

    masks = (core, occ_mask, virt_mask, three_mask)
    one, two, near, late = call(
        pack_kernel, "pack",
        [shape(tile + 16, 5 * tile), shape(tile, 2 * tile)] + [shape(half, height, tile)] * 2,
        [SMEM] * 4 + [VMEM] * 3, [VMEM] * 2 + [ANY] * 2,
        scratch_shapes=[pltpu.SemaphoreType.DMA((2,))],
    )(*masks, occ_band, virt_band, three_center)
    one_hop = lax.ppermute(one, BOTH, mixed((1, 0), (-1, 0)))
    two_hops = shifted(two, "ao", -2)
    halo_near, far_near = shifted(near, "ao", -1), shifted(near, "ri", 2)
    halo_late = shifted(late, "ao", -1)
    late, _ = lax.optimization_barrier((late, two_hops))
    far_late = shifted(late, "ri", 2)

    one_hop, _ = lax.optimization_barrier((one_hop, two_hops))
    joined = partner(one_hop)
    flat = relayout(joined, three_center)
    early, places = [flat, partner(flat)], [mine, mine ^ 1]
    for distance in range(2, groups // 2):
        step = shifted(flat, "ri", 2 * distance)
        early += [step, partner(step)]
        places += [(mine - 2 * distance) % groups, ((mine ^ 1) - 2 * distance) % groups]
    places += [(mine - 2) % groups, ((mine ^ 1) - 2) % groups]
    places = jnp.stack(places).astype(jnp.int32)

    green_own, green_halo, virt_own, virt_next = call(
        tables_kernel, "tables",
        [shape(3 * tile, 3 * tile), shape(6 * tile, 3 * tile), shape(tile, 2 * tile), shape(tile, tile)],
        [SMEM] * 4 + [VMEM] * 5 + [ANY], [VMEM] * 4,
        scratch_shapes=[
            pltpu.VMEM((tile + 16, 5 * tile), BF16),
            pltpu.VMEM((tile + 16, 5 * tile), BF16),
        ],
    )(*masks, occ_band, virt_band, one_hop, two_hops, joined, flat)
    m_near, m_late = own_m(green_own, three_center)
    greens = (green_halo, virt_own, virt_next)

    halo_near, far_near, _ = lax.optimization_barrier((halo_near, far_near, m_near))
    passed = partner(far_near)
    panels_near = halo_panels(m_late, halo_near, m_near, *greens)
    far_near = far_rows(panels_near, far_near, passed)

    halo_late, far_late, _ = lax.optimization_barrier((halo_late, far_late, far_near))
    passed = partner(far_late)
    panels_late = halo_panels(far_near, halo_late, m_late, *greens)
    far_late = far_rows(panels_late, far_late, passed)
    parts = contract(places, [panels_near, panels_late], early + [far_near, far_late], lines)
    swapped = lax.all_to_all(parts.reshape(lines * groups, *parts.shape[2:]), BOTH, 0, 0, tiled=True)
    return call(total_kernel, "total", shape(batch, groups * batch, dtype=F32), [VMEM])(swapped)


def solution(mesh):
    placed = (P("ri", "ao", None),) + (P("ao", None),) * 5
    return jax.shard_map(
        per_device, mesh=mesh, in_specs=placed, out_specs=P("ri", None), check_vma=False
    )
```

```python
import functools

import jax
import jax.numpy as jnp
from jax import lax
from jax.experimental import pallas as pl
from jax.experimental.pallas import tpu as pltpu
from jax.sharding import PartitionSpec as P

F32, BF16 = jnp.float32, jnp.bfloat16
MIB = 1024 * 1024
ANY = pl.BlockSpec(memory_space=pl.ANY)
VMEM = pl.BlockSpec(memory_space=pltpu.VMEM)
SMEM = pl.BlockSpec(memory_space=pltpu.SMEM)
BOTH = ("ao", "ri")
LARGE = pl.CostEstimate(flops=10**11, bytes_accessed=10**9, transcendentals=0)
LITTLE = pl.CostEstimate(flops=1024, bytes_accessed=1024, transcendentals=0)


def call(kernel, name, out_shape, in_specs, out_specs=VMEM, room=16, **more):
    return pl.pallas_call(
        kernel,
        name=name,
        out_shape=out_shape,
        in_specs=in_specs,
        out_specs=out_specs,
        compiler_params=pltpu.CompilerParams(vmem_limit_bytes=room * MIB),
        cost_estimate=LARGE if name in ("relayout",) else LITTLE,
        **more,
    )


def shape(*dims, dtype=BF16):
    return jax.ShapeDtypeStruct(dims, dtype)


def dot_nn(a, b, **more):
    return lax.dot_general(a, b, (((1,), (0,)), ((), ())), preferred_element_type=F32, **more)


def dot_nt(a, b):
    return lax.dot_general(a, b, (((1,), (1,)), ((), ())), preferred_element_type=F32)


def when_core(core, even, odd):
    pl.when(core == 0)(even)
    pl.when(core != 0)(odd)


def pack_kernel(mine_ref, occ_mask, virt_mask, three_mask, occ_ref, virt_ref, one_ref, two_ref):
    tile = occ_ref.shape[0]

    def cols(k):
        return slice(k * tile, (k + 1) * tile)

    occ = [occ_ref[:, cols(k)] * occ_mask[0, k].astype(BF16) for k in range(5)]

    def even():
        for k in range(4):
            one_ref[:tile, cols(k)] = occ[k]
        one_ref[:tile, cols(4)] = virt_ref[:, :tile] * virt_mask[0, 0].astype(BF16)

    def odd():
        for k in range(3):
            one_ref[:tile, cols(k)] = occ[k + 2]
        one_ref[:tile, 3 * tile :] = jnp.zeros((tile, 2 * tile), BF16)

    when_core(lax.rem(mine_ref[0], 2), even, odd)
    one_ref[tile:, :] = jnp.zeros((16, 5 * tile), BF16)
    for k in range(3):
        flag = jnp.full((16, tile), three_mask[0, k].astype(F32), F32)
        one_ref[tile:, cols(k)] = flag.astype(BF16)
    for k in range(2):
        two_ref[:, cols(k)] = occ[k]


def half_kernel(which, after_ref, src_ref, out_ref, held, sems):
    half = out_ref.shape[0]
    quarter = half // 2
    moves = []
    for k in range(2):
        rows = slice(k * quarter, (k + 1) * quarter)
        source = src_ref.at[which * half + k * quarter : which * half + (k + 1) * quarter]
        moves.append((
            pltpu.make_async_copy(source, held.at[rows], sems.at[k]),
            pltpu.make_async_copy(held.at[rows], out_ref.at[rows], sems.at[2 + k]),
        ))
    for load, _ in moves:
        load.start()
    for load, store in moves:
        load.wait()
        store.start()
    for _, store in moves:
        store.wait()


def half_of(which, after, src):
    dims = (src.shape[0] // 2, *src.shape[1:])
    return call(
        functools.partial(half_kernel, which), ("half_near", "half_late")[which], shape(*dims), [ANY] * 2, ANY, room=56,
        scratch_shapes=[pltpu.VMEM(dims, BF16), pltpu.SemaphoreType.DMA((4,))],
    )(after, src)


def tables_kernel(
    mine_ref, occ_mask, virt_mask, three_mask, occ_ref, virt_ref, one_ref, other_ref, upper2, after_ref,
    own_ref, halo_ref, virt_own_ref, virt_next_ref, lower, upper,
):
    tile = occ_ref.shape[0]

    def even():
        lower[...], upper[...] = other_ref[...], one_ref[...]

    def odd():
        lower[...], upper[...] = one_ref[...], other_ref[...]

    when_core(lax.rem(mine_ref[0], 2), even, odd)

    def cols(k):
        return slice(k * tile, (k + 1) * tile)

    def entry(mu, lam):
        if abs(mu - lam) > 2:
            return None
        if mu == -1:
            return lower[:tile, cols(lam + 1)]
        if mu == 0:
            return occ_ref[:, cols(lam + 2)] * occ_mask[0, lam + 2].astype(BF16)
        if mu == 1:
            return upper[:tile, cols(lam + 1)]
        return upper2[:, cols(lam)]

    blank = jnp.zeros((tile, tile), BF16)
    own = [three_mask[0, k].astype(BF16) for k in range(3)]
    after = [upper[tile : tile + 1, cols(k)] for k in range(3)]
    for lam in range(-1, 2):
        for mu in range(-1, 3):
            block = entry(mu, lam)
            if block is not None:
                block = block.T * own[lam + 1]
            if mu < 2:
                own_ref[cols(lam + 1), cols(mu + 1)] = block * own[mu + 1]
            if mu > -1:
                halo_ref[cols(lam + 1), cols(mu)] = blank if block is None else block * after[mu]
    for mu in range(-1, 2):
        for lam in range(3):
            block = entry(mu, lam)
            value = blank if block is None else block * own[mu + 1] * after[lam]
            halo_ref[cols(mu + 4), cols(lam)] = value
    for k in range(2):
        virt_own_ref[:, cols(k)] = virt_ref[:, cols(k + 1)] * virt_mask[0, k + 1].astype(BF16)
    virt_next_ref[...] = upper[:tile, 4 * tile :]


def relayout_kernel(after_ref, src_ref, out_ref):
    out_ref[...] = jnp.swapaxes(src_ref[...], 0, 1)


def relayout(after, src, steps=3):
    batch, height, width = src.shape
    part = height // steps
    return call(
        relayout_kernel, "relayout", shape(height, batch, width),
        [ANY, pl.BlockSpec((batch, part, width), lambda i: (0, i, 0))],
        pl.BlockSpec((part, batch, width), lambda i: (i, 0, 0)),
        grid=(steps,),
    )(after, src)


def far_kernel(after_ref, near_ref, other_ref, out_ref, held, sems):
    batch, height, width = held.shape[1:]
    moves = [
        pltpu.make_async_copy(ref, held.at[k], sems.at[k])
        for k, ref in enumerate((near_ref, other_ref))
    ]
    for move in moves:
        move.start()
    for move in moves:
        move.wait()
    out_ref[...] = jnp.swapaxes(held[...].reshape(2 * batch, height, width), 0, 1)


def far_rows(after, near, other):
    batch, height, width = near.shape
    return call(
        far_kernel, "far_rows", shape(height, 2 * batch, width), [ANY] * 3,
        scratch_shapes=[
            pltpu.VMEM((2, batch, height, width), BF16),
            pltpu.SemaphoreType.DMA((2,)),
        ],
    )(after, near, other)


def own_m_kernel(green_ref, src_ref, *rest):
    outs, wide = rest[:2], rest[2]
    batch, _, width = src_ref.shape
    height, half = green_ref.shape[0], batch // 2
    for k, out_ref in enumerate(outs):
        for p in range(0, half, 2):
            pair = jnp.concatenate([src_ref[k * half + p], src_ref[k * half + p + 1]], 1)
            both = dot_nn(green_ref[...], pair)
            wide[k, pl.ds(p, height, half), :] = both[:, :width]
            wide[k, pl.ds(p + 1, height, half), :] = both[:, width:]
        out_ref[...] = wide[k].astype(BF16)


def own_m(green, src):
    batch, height, width = src.shape
    rows = width * batch // 2
    return call(
        own_m_kernel, "own_m", [shape(height * batch // 2, width)] * 2,
        [
            pl.BlockSpec((width, height), lambda i: (i, 0)),
            pl.BlockSpec((batch, height, width), lambda i: (0, 0, 0)),
        ],
        [pl.BlockSpec((rows, width), lambda i: (i, 0))] * 2,
        grid=(height // width,),
        scratch_shapes=[pltpu.VMEM((2, rows, width), F32)],
    )(green, src)


def halo_kernel(
    after_ref, halo_ref, m_ref, green_ref, virt_own_ref, virt_next_ref, out_ref,
    held, m_own, wide_m, wide_u, sems,
):
    batch, height, width = held.shape
    halo_move = pltpu.make_async_copy(halo_ref, held, sems.at[0])
    halo_move.start()
    m_move = pltpu.make_async_copy(m_ref, m_own, sems.at[1])
    m_move.start()
    halo_move.wait()
    for p in range(0, batch, 2):
        pair = jnp.concatenate([held[p], held[p + 1]], 1)
        both = dot_nn(green_ref[...], pair)
        wide_m[pl.ds(p, height, batch), :] = both[:height, :width]
        wide_m[pl.ds(p + 1, height, batch), :] = both[:height, width:]
        wide_u[pl.ds(p, height, batch), :] = both[height:, :width]
        wide_u[pl.ds(p + 1, height, batch), :] = both[height:, width:]
    m_move.wait()
    group = height // 6

    def second_stage(step, carry):
        at = pl.multiple_of(step * group, group)
        rows = pl.ds(pl.multiple_of(at * batch, group * batch), group * batch)
        both = jnp.concatenate([m_own[rows, :], wide_m[rows, :].astype(BF16)], 1)
        x = dot_nt(both, virt_own_ref[...]).reshape(group, batch, width)
        v = dot_nn(wide_u[rows, :].astype(BF16), virt_next_ref[...]).reshape(group, batch, width)
        out_ref[pl.ds(at, group)] = jnp.concatenate([x, v], 1).astype(BF16)
        return carry

    lax.fori_loop(0, height // group, second_stage, 0)


def halo_panels(name, after, halo, m_own, green, virt_own, virt_next):
    batch, height, width = halo.shape
    return call(
        halo_kernel, name, shape(height, 2 * batch, width),
        [ANY] * 3 + [VMEM] * 3,
        scratch_shapes=[
            pltpu.VMEM((batch, height, width), BF16),
            pltpu.VMEM((height * batch, width), BF16),
            pltpu.VMEM((height * batch, width), F32),
            pltpu.VMEM((height * batch, width), F32),
            pltpu.SemaphoreType.DMA((2,)),
        ],
    )(after, halo, m_own, green, virt_own, virt_next)


def contract_kernel(lefts, rights, group, distances, mine_ref, *refs):
    out_ref, total_ref = refs[-2:]
    left, right = refs[:lefts], refs[lefts : lefts + rights]
    step, steps = pl.program_id(0), pl.num_programs(0)

    @pl.when(step == 0)
    def _():
        total_ref[...] = jnp.zeros_like(total_ref)

    total = None
    for at in range(0, left[0].shape[0], group):
        sides = [
            jnp.concatenate(
                [jnp.concatenate([ref[at + k] for k in range(group)], 1) for ref in side], 0
            )
            for side in (left, right)
        ]
        part = dot_nt(*sides)
        total = part if total is None else total + part
    total_ref[...] += total

    @pl.when(step == steps - 1)
    def _():
        lines, chunks, deep, wide = out_ref.shape
        rows, cols = total_ref.shape
        batch = rows // 2
        half = batch // 2
        exact = dict(precision=lax.Precision.HIGHEST)
        source = lax.broadcasted_iota(jnp.int32, (cols, cols), 0)
        target = lax.broadcasted_iota(jnp.int32, (cols, cols), 1)
        block, within = source // batch, source % batch
        place = jnp.zeros((cols, cols), jnp.int32)
        groups, mine = cols // batch, mine_ref[0]
        for k, distance in enumerate(distances):
            for j, device in enumerate((mine, mine + 1 - 2 * lax.rem(mine, 2))):
                start = lax.rem(device - 2 * distance + groups, groups) * batch
                place = jnp.where(block == 2 * k + j, start + within, place)
        spread = jnp.where(place == target, 1.0, 0.0).astype(F32)
        placed = dot_nn(total_ref[...], spread, **exact)

        row = lax.broadcasted_iota(jnp.int32, (cols, rows), 0) - mine * batch
        have = lax.broadcasted_iota(jnp.int32, (cols, rows), 1)
        chunk, part, index = have // batch, have % batch // half, have % half
        at = (row == chunk * half + index) & (row >= 0) & (row < batch)
        pick_x = jnp.where(at & (part == 0), 1.0, 0.0).astype(F32)
        pick_v = jnp.where(at & (part == 1), 1.0, 0.0).astype(F32)
        result = dot_nn(pick_x, placed, **exact) + dot_nn(pick_v, placed, **exact).T
        fold = batch // deep
        for k in range(chunks):
            piece = jnp.concatenate(
                [result[k * batch + j * deep : k * batch + (j + 1) * deep] for j in range(fold)], 1
            )
            for line in range(lines):
                out_ref[line, k] = piece


def contract(mine, distances, lefts, rights, lines, steps=3):
    height, _, width = lefts[0].shape
    part = height // steps
    rows, cols = [sum(a.shape[1] for a in side) for side in (lefts, rights)]
    batch = rows // 2
    fold = max(1, width // cols)
    dims = (lines, cols // batch, batch // fold, cols * fold)
    return call(
        functools.partial(contract_kernel, len(lefts), len(rights), 16, distances), "contract",
        shape(*dims, dtype=F32),
        [SMEM] + [pl.BlockSpec((part, a.shape[1], width), lambda i: (i, 0, 0)) for a in lefts + rights],
        pl.BlockSpec(dims, lambda i: (0, 0, 0, 0)),
        grid=(steps,),
        scratch_shapes=[pltpu.VMEM((rows, cols), F32)],
    )(mine, *lefts, *rights)


def total_kernel(src_ref, out_ref):
    total = -jnp.sum(src_ref[...], 0)
    deep, cols = total.shape[0], out_ref.shape[1]
    for j in range(out_ref.shape[0] // deep):
        out_ref[j * deep : (j + 1) * deep, :] = total[:, j * cols : (j + 1) * cols]


def shifted(value, axis, distance):
    size = lax.axis_size(axis)
    return lax.ppermute(value, axis, [(i, (i + distance) % size) for i in range(size)])


def per_device(three_center, occ_band, virt_band, three_mask, occ_mask, virt_mask):
    batch, height, tile = three_center.shape
    lines, groups = lax.axis_size("ao"), lax.axis_size("ri")
    mine = lax.axis_index("ri").astype(jnp.int32)[None]
    half = batch // 2

    def mixed(near, far):
        pairs = []
        for a in range(lines):
            for r in range(groups):
                da, dr = near if r % 2 else far
                pairs.append((a * groups + r, ((a + da) % lines) * groups + (r + dr) % groups))
        return pairs

    def partner(value):
        return lax.ppermute(value, "ri", [(i, i ^ 1) for i in range(groups)])

    masks = (mine, occ_mask, virt_mask, three_mask)
    far = shifted(three_center, "ri", 2)
    one, two = call(
        pack_kernel, "pack", [shape(tile + 16, 5 * tile), shape(tile, 2 * tile)],
        [SMEM] * 4 + [VMEM] * 2, [VMEM] * 2, room=56,
    )(*masks, occ_band, virt_band)
    one_hop, two_hops = lax.ppermute(one, BOTH, mixed((1, 0), (-1, 0))), shifted(two, "ao", -2)
    near = half_of(0, one, three_center)
    halo_near = shifted(near, "ao", -1)
    late = half_of(1, near, three_center)
    halo_late = shifted(late, "ao", -1)
    flat = relayout(late, three_center)
    halo_late = shifted(late, "ao", -1)
    early, distances = [flat, partner(flat)], [0]
    for distance in range(2, groups // 2):
        step = shifted(flat, "ri", 2 * distance)
        early += [step, partner(step)]
        distances.append(distance)

    one_hop, two_hops, _ = lax.optimization_barrier((one_hop, two_hops, flat))
    green_own, green_halo, virt_own, virt_next = call(
        tables_kernel, "tables",
        [shape(3 * tile, 3 * tile), shape(6 * tile, 3 * tile), shape(tile, 2 * tile), shape(tile, tile)],
        [SMEM] * 4 + [VMEM] * 5 + [ANY], [VMEM] * 4,
        scratch_shapes=[pltpu.VMEM((tile + 16, 5 * tile), BF16)] * 2,
    )(*masks, occ_band, virt_band, one_hop, partner(one_hop), two_hops, flat)
    m_near, m_late = own_m(green_own, three_center)
    greens = (green_halo, virt_own, virt_next)

    halo_near, _ = lax.optimization_barrier((halo_near, m_near))
    panels_near = halo_panels("halo_near", m_late, halo_near, m_near, *greens)
    halo_late, far, _ = lax.optimization_barrier((halo_late, far, panels_near))
    passed = partner(far)
    panels_late = halo_panels("halo_late", panels_near, halo_late, m_late, *greens)
    far_all = far_rows(panels_late, far, passed)
    parts = contract(mine, distances + [1], [panels_near, panels_late], early + [far_all], lines)
    swapped = lax.all_to_all(parts.reshape(lines * groups, *parts.shape[2:]), BOTH, 0, 0, tiled=True)
    return call(total_kernel, "total", shape(batch, groups * batch, dtype=F32), [VMEM])(swapped)


def solution(mesh):
    placed = (P("ri", "ao", None),) + (P("ao", None),) * 5
    return jax.shard_map(
        per_device, mesh=mesh, in_specs=placed, out_specs=P("ri", None), check_vma=False
    )
```

```python
import functools

import jax
import jax.numpy as jnp
from jax import lax
from jax.experimental import pallas as pl
from jax.experimental.pallas import tpu as pltpu
from jax.sharding import PartitionSpec as P

F32, BF16 = jnp.float32, jnp.bfloat16
MIB = 1024 * 1024
ANY = pl.BlockSpec(memory_space=pl.ANY)
VMEM = pl.BlockSpec(memory_space=pltpu.VMEM)
SMEM = pl.BlockSpec(memory_space=pltpu.SMEM)
BOTH = ("ao", "ri")
LARGE = pl.CostEstimate(flops=10**11, bytes_accessed=10**9, transcendentals=0)
LITTLE = pl.CostEstimate(flops=1024, bytes_accessed=1024, transcendentals=0)


def call(kernel, name, out_shape, in_specs, out_specs=VMEM, room=16, **more):
    return pl.pallas_call(
        kernel,
        name=name,
        out_shape=out_shape,
        in_specs=in_specs,
        out_specs=out_specs,
        compiler_params=pltpu.CompilerParams(vmem_limit_bytes=room * MIB),
        cost_estimate=LARGE if name in ("halo_near", "half_late") else LITTLE,
        **more,
    )


def shape(*dims, dtype=BF16):
    return jax.ShapeDtypeStruct(dims, dtype)


def dot_nn(a, b, **more):
    return lax.dot_general(a, b, (((1,), (0,)), ((), ())), preferred_element_type=F32, **more)


def dot_nt(a, b):
    return lax.dot_general(a, b, (((1,), (1,)), ((), ())), preferred_element_type=F32)


def when_core(core, even, odd):
    pl.when(core == 0)(even)
    pl.when(core != 0)(odd)


def pack_kernel(mine_ref, occ_mask, virt_mask, three_mask, occ_ref, virt_ref, one_ref, two_ref):
    tile = occ_ref.shape[0]

    def cols(k):
        return slice(k * tile, (k + 1) * tile)

    occ = [occ_ref[:, cols(k)] * occ_mask[0, k].astype(BF16) for k in range(5)]

    def even():
        for k in range(4):
            one_ref[:tile, cols(k)] = occ[k]
        one_ref[:tile, cols(4)] = virt_ref[:, :tile] * virt_mask[0, 0].astype(BF16)

    def odd():
        for k in range(3):
            one_ref[:tile, cols(k)] = occ[k + 2]
        one_ref[:tile, 3 * tile :] = jnp.zeros((tile, 2 * tile), BF16)

    when_core(lax.rem(mine_ref[0], 2), even, odd)
    one_ref[tile:, :] = jnp.zeros((16, 5 * tile), BF16)
    for k in range(3):
        flag = jnp.full((16, tile), three_mask[0, k].astype(F32), F32)
        one_ref[tile:, cols(k)] = flag.astype(BF16)
    for k in range(2):
        two_ref[:, cols(k)] = occ[k]


def half_kernel(which, after_ref, src_ref, out_ref, held, sems):
    half = out_ref.shape[0]
    quarter = half // 2
    moves = []
    for k in range(2):
        rows = slice(k * quarter, (k + 1) * quarter)
        source = src_ref.at[which * half + k * quarter : which * half + (k + 1) * quarter]
        moves.append((
            pltpu.make_async_copy(source, held.at[rows], sems.at[k]),
            pltpu.make_async_copy(held.at[rows], out_ref.at[rows], sems.at[2 + k]),
        ))
    for load, _ in moves:
        load.start()
    for load, store in moves:
        load.wait()
        store.start()
    for _, store in moves:
        store.wait()


def half_of(which, after, src):
    dims = (src.shape[0] // 2, *src.shape[1:])
    return call(
        functools.partial(half_kernel, which), ("half_near", "half_late")[which], shape(*dims), [ANY] * 2, ANY, room=56,
        scratch_shapes=[pltpu.VMEM(dims, BF16), pltpu.SemaphoreType.DMA((4,))],
    )(after, src)


def tables_kernel(
    mine_ref, occ_mask, virt_mask, three_mask, occ_ref, virt_ref, one_ref, other_ref, upper2, after_ref,
    own_ref, halo_ref, virt_own_ref, virt_next_ref, lower, upper,
):
    tile = occ_ref.shape[0]

    def even():
        lower[...], upper[...] = other_ref[...], one_ref[...]

    def odd():
        lower[...], upper[...] = one_ref[...], other_ref[...]

    when_core(lax.rem(mine_ref[0], 2), even, odd)

    def cols(k):
        return slice(k * tile, (k + 1) * tile)

    def entry(mu, lam):
        if abs(mu - lam) > 2:
            return None
        if mu == -1:
            return lower[:tile, cols(lam + 1)]
        if mu == 0:
            return occ_ref[:, cols(lam + 2)] * occ_mask[0, lam + 2].astype(BF16)
        if mu == 1:
            return upper[:tile, cols(lam + 1)]
        return upper2[:, cols(lam)]

    blank = jnp.zeros((tile, tile), BF16)
    own = [three_mask[0, k].astype(BF16) for k in range(3)]
    after = [upper[tile : tile + 1, cols(k)] for k in range(3)]
    for lam in range(-1, 2):
        for mu in range(-1, 3):
            block = entry(mu, lam)
            if block is not None:
                block = block.T * own[lam + 1]
            if mu < 2:
                own_ref[cols(lam + 1), cols(mu + 1)] = block * own[mu + 1]
            if mu > -1:
                halo_ref[cols(lam + 1), cols(mu)] = blank if block is None else block * after[mu]
    for mu in range(-1, 2):
        for lam in range(3):
            block = entry(mu, lam)
            value = blank if block is None else block * own[mu + 1] * after[lam]
            halo_ref[cols(mu + 4), cols(lam)] = value
    for k in range(2):
        virt_own_ref[:, cols(k)] = virt_ref[:, cols(k + 1)] * virt_mask[0, k + 1].astype(BF16)
    virt_next_ref[...] = upper[:tile, 4 * tile :]


def relayout_kernel(after_ref, src_ref, out_ref):
    out_ref[...] = jnp.swapaxes(src_ref[...], 0, 1)


def relayout(after, src, steps=3):
    batch, height, width = src.shape
    part = height // steps
    return call(
        relayout_kernel, "relayout", shape(height, batch, width),
        [ANY, pl.BlockSpec((batch, part, width), lambda i: (0, i, 0))],
        pl.BlockSpec((part, batch, width), lambda i: (i, 0, 0)),
        grid=(steps,),
    )(after, src)


def far_kernel(after_ref, near_ref, other_ref, out_ref, held, sems):
    batch, height, width = held.shape[1:]
    moves = [
        pltpu.make_async_copy(ref, held.at[k], sems.at[k])
        for k, ref in enumerate((near_ref, other_ref))
    ]
    for move in moves:
        move.start()
    for move in moves:
        move.wait()
    out_ref[...] = jnp.swapaxes(held[...].reshape(2 * batch, height, width), 0, 1)


def far_rows(after, near, other):
    batch, height, width = near.shape
    return call(
        far_kernel, "far_rows", shape(height, 2 * batch, width), [ANY] * 3,
        scratch_shapes=[
            pltpu.VMEM((2, batch, height, width), BF16),
            pltpu.SemaphoreType.DMA((2,)),
        ],
    )(after, near, other)


def own_m_kernel(green_ref, src_ref, *rest):
    outs, wide = rest[:2], rest[2]
    batch, _, width = src_ref.shape
    height, half = green_ref.shape[0], batch // 2
    for k, out_ref in enumerate(outs):
        for p in range(0, half, 2):
            pair = jnp.concatenate([src_ref[k * half + p], src_ref[k * half + p + 1]], 1)
            both = dot_nn(green_ref[...], pair)
            wide[k, pl.ds(p, height, half), :] = both[:, :width]
            wide[k, pl.ds(p + 1, height, half), :] = both[:, width:]
        out_ref[...] = wide[k].astype(BF16)


def own_m(green, src):
    batch, height, width = src.shape
    rows = width * batch // 2
    return call(
        own_m_kernel, "own_m", [shape(height * batch // 2, width)] * 2,
        [
            pl.BlockSpec((width, height), lambda i: (i, 0)),
            pl.BlockSpec((batch, height, width), lambda i: (0, 0, 0)),
        ],
        [pl.BlockSpec((rows, width), lambda i: (i, 0))] * 2,
        grid=(height // width,),
        scratch_shapes=[pltpu.VMEM((2, rows, width), F32)],
    )(green, src)


def halo_kernel(
    after_ref, halo_ref, m_ref, green_ref, virt_own_ref, virt_next_ref, out_ref,
    held, m_own, wide_m, wide_u, sems,
):
    batch, height, width = held.shape
    halo_move = pltpu.make_async_copy(halo_ref, held, sems.at[0])
    halo_move.start()
    m_move = pltpu.make_async_copy(m_ref, m_own, sems.at[1])
    m_move.start()
    halo_move.wait()
    for p in range(0, batch, 2):
        pair = jnp.concatenate([held[p], held[p + 1]], 1)
        both = dot_nn(green_ref[...], pair)
        wide_m[pl.ds(p, height, batch), :] = both[:height, :width]
        wide_m[pl.ds(p + 1, height, batch), :] = both[:height, width:]
        wide_u[pl.ds(p, height, batch), :] = both[height:, :width]
        wide_u[pl.ds(p + 1, height, batch), :] = both[height:, width:]
    m_move.wait()
    group = height // 6

    for at in range(0, height, group):
        rows = pl.ds(at * batch, group * batch)
        both = jnp.concatenate([m_own[rows, :], wide_m[rows, :].astype(BF16)], 1)
        x = dot_nt(both, virt_own_ref[...]).reshape(group, batch, width)
        v = dot_nn(wide_u[rows, :].astype(BF16), virt_next_ref[...]).reshape(group, batch, width)
        out_ref[at : at + group] = jnp.concatenate([x, v], 1).astype(BF16)


def halo_panels(name, after, halo, m_own, green, virt_own, virt_next):
    batch, height, width = halo.shape
    return call(
        halo_kernel, name, shape(height, 2 * batch, width),
        [ANY] * 3 + [VMEM] * 3,
        scratch_shapes=[
            pltpu.VMEM((batch, height, width), BF16),
            pltpu.VMEM((height * batch, width), BF16),
            pltpu.VMEM((height * batch, width), F32),
            pltpu.VMEM((height * batch, width), F32),
            pltpu.SemaphoreType.DMA((2,)),
        ],
    )(after, halo, m_own, green, virt_own, virt_next)


def contract_kernel(lefts, rights, group, distances, mine_ref, *refs):
    out_ref, total_ref = refs[-2:]
    left, right = refs[:lefts], refs[lefts : lefts + rights]
    step, steps = pl.program_id(0), pl.num_programs(0)

    @pl.when(step == 0)
    def _():
        total_ref[...] = jnp.zeros_like(total_ref)

    total = None
    for at in range(0, left[0].shape[0], group):
        sides = [
            jnp.concatenate(
                [jnp.concatenate([ref[at + k] for k in range(group)], 1) for ref in side], 0
            )
            for side in (left, right)
        ]
        part = dot_nt(*sides)
        total = part if total is None else total + part
    total_ref[...] += total

    @pl.when(step == steps - 1)
    def _():
        lines, chunks, deep, wide = out_ref.shape
        rows, cols = total_ref.shape
        batch = rows // 2
        half = batch // 2
        exact = dict(precision=lax.Precision.HIGHEST)
        source = lax.broadcasted_iota(jnp.int32, (cols, cols), 0)
        target = lax.broadcasted_iota(jnp.int32, (cols, cols), 1)
        block, within = source // batch, source % batch
        place = jnp.zeros((cols, cols), jnp.int32)
        groups, mine = cols // batch, mine_ref[0]
        for k, distance in enumerate(distances):
            for j, device in enumerate((mine, mine + 1 - 2 * lax.rem(mine, 2))):
                start = lax.rem(device - 2 * distance + groups, groups) * batch
                place = jnp.where(block == 2 * k + j, start + within, place)
        spread = jnp.where(place == target, 1.0, 0.0).astype(F32)
        placed = dot_nn(total_ref[...], spread, **exact)

        row = lax.broadcasted_iota(jnp.int32, (cols, rows), 0) - mine * batch
        have = lax.broadcasted_iota(jnp.int32, (cols, rows), 1)
        chunk, part, index = have // batch, have % batch // half, have % half
        at = (row == chunk * half + index) & (row >= 0) & (row < batch)
        pick_x = jnp.where(at & (part == 0), 1.0, 0.0).astype(F32)
        pick_v = jnp.where(at & (part == 1), 1.0, 0.0).astype(F32)
        result = dot_nn(pick_x, placed, **exact) + dot_nn(pick_v, placed, **exact).T
        fold = batch // deep
        for k in range(chunks):
            piece = jnp.concatenate(
                [result[k * batch + j * deep : k * batch + (j + 1) * deep] for j in range(fold)], 1
            )
            for line in range(lines):
                out_ref[line, k] = piece


def contract(mine, distances, lefts, rights, lines, steps=3):
    height, _, width = lefts[0].shape
    part = height // steps
    rows, cols = [sum(a.shape[1] for a in side) for side in (lefts, rights)]
    batch = rows // 2
    fold = max(1, width // cols)
    dims = (lines, cols // batch, batch // fold, cols * fold)
    return call(
        functools.partial(contract_kernel, len(lefts), len(rights), 16, distances), "contract",
        shape(*dims, dtype=F32),
        [SMEM] + [pl.BlockSpec((part, a.shape[1], width), lambda i: (i, 0, 0)) for a in lefts + rights],
        pl.BlockSpec(dims, lambda i: (0, 0, 0, 0)),
        grid=(steps,),
        scratch_shapes=[pltpu.VMEM((rows, cols), F32)],
    )(mine, *lefts, *rights)


def total_kernel(src_ref, out_ref):
    total = -jnp.sum(src_ref[...], 0)
    deep, cols = total.shape[0], out_ref.shape[1]
    for j in range(out_ref.shape[0] // deep):
        out_ref[j * deep : (j + 1) * deep, :] = total[:, j * cols : (j + 1) * cols]


def shifted(value, axis, distance):
    size = lax.axis_size(axis)
    return lax.ppermute(value, axis, [(i, (i + distance) % size) for i in range(size)])


def per_device(three_center, occ_band, virt_band, three_mask, occ_mask, virt_mask):
    batch, height, tile = three_center.shape
    lines, groups = lax.axis_size("ao"), lax.axis_size("ri")
    mine = lax.axis_index("ri").astype(jnp.int32)[None]
    half = batch // 2

    def mixed(near, far):
        pairs = []
        for a in range(lines):
            for r in range(groups):
                da, dr = near if r % 2 else far
                pairs.append((a * groups + r, ((a + da) % lines) * groups + (r + dr) % groups))
        return pairs

    def partner(value):
        return lax.ppermute(value, "ri", [(i, i ^ 1) for i in range(groups)])

    masks = (mine, occ_mask, virt_mask, three_mask)
    far = shifted(three_center, "ri", 2)
    one, two = call(
        pack_kernel, "pack", [shape(tile + 16, 5 * tile), shape(tile, 2 * tile)],
        [SMEM] * 4 + [VMEM] * 2, [VMEM] * 2, room=56,
    )(*masks, occ_band, virt_band)
    one_hop, two_hops = lax.ppermute(one, BOTH, mixed((1, 0), (-1, 0))), shifted(two, "ao", -2)
    near = half_of(0, one, three_center)
    halo_near = shifted(near, "ao", -1)
    late = half_of(1, near, three_center)
    halo_late = shifted(late, "ao", -1)
    flat = relayout(late, three_center)
    one_hop, two_hops, _ = lax.optimization_barrier((one_hop, two_hops, flat))
    green_own, green_halo, virt_own, virt_next = call(
        tables_kernel, "tables",
        [shape(3 * tile, 3 * tile), shape(6 * tile, 3 * tile), shape(tile, 2 * tile), shape(tile, tile)],
        [SMEM] * 4 + [VMEM] * 5 + [ANY], [VMEM] * 4,
        scratch_shapes=[pltpu.VMEM((tile + 16, 5 * tile), BF16)] * 2,
    )(*masks, occ_band, virt_band, one_hop, partner(one_hop), two_hops, flat)
    m_near, m_late = own_m(green_own, three_center)
    early, distances = [flat, partner(lax.optimization_barrier((flat, m_near))[0])], [0]
    for distance in range(2, groups // 2):
        step = shifted(flat, "ri", 2 * distance)
        early += [step, partner(step)]
        distances.append(distance)

    greens = (green_halo, virt_own, virt_next)

    halo_near, _ = lax.optimization_barrier((halo_near, m_near))
    panels_near = halo_panels("halo_near", m_late, halo_near, m_near, *greens)
    far, _ = lax.optimization_barrier((far, m_near))
    passed = partner(far)
    far_all = far_rows(panels_near, far, passed)
    halo_late, _ = lax.optimization_barrier((halo_late, far_all))
    panels_late = halo_panels("halo_late", early[1], halo_late, m_late, *greens)
    parts = contract(mine, distances + [1], [panels_near, panels_late], early + [far_all], lines)
    swapped = lax.all_to_all(parts.reshape(lines * groups, *parts.shape[2:]), BOTH, 0, 0, tiled=True)
    return call(total_kernel, "total", shape(batch, groups * batch, dtype=F32), [VMEM])(swapped)


def solution(mesh):
    placed = (P("ri", "ao", None),) + (P("ao", None),) * 5
    return jax.shard_map(
        per_device, mesh=mesh, in_specs=placed, out_specs=P("ri", None), check_vma=False
    )
```

```python
import functools

import jax
import jax.numpy as jnp
from jax import lax
from jax.experimental import pallas as pl
from jax.experimental.pallas import tpu as pltpu
from jax.sharding import PartitionSpec as P

F32, BF16 = jnp.float32, jnp.bfloat16
MIB = 1024 * 1024
ANY = pl.BlockSpec(memory_space=pl.ANY)
VMEM = pl.BlockSpec(memory_space=pltpu.VMEM)
SMEM = pl.BlockSpec(memory_space=pltpu.SMEM)
BOTH = ("ao", "ri")
LARGE = pl.CostEstimate(flops=10**11, bytes_accessed=10**9, transcendentals=0)
LITTLE = pl.CostEstimate(flops=1024, bytes_accessed=1024, transcendentals=0)


def call(kernel, name, out_shape, in_specs, out_specs=VMEM, room=16, **more):
    return pl.pallas_call(
        kernel,
        name=name,
        out_shape=out_shape,
        in_specs=in_specs,
        out_specs=out_specs,
        compiler_params=pltpu.CompilerParams(vmem_limit_bytes=room * MIB),
        cost_estimate=LARGE if name in ("halo_near", "half_late") else LITTLE,
        **more,
    )


def shape(*dims, dtype=BF16):
    return jax.ShapeDtypeStruct(dims, dtype)


def dot_nn(a, b, **more):
    return lax.dot_general(a, b, (((1,), (0,)), ((), ())), preferred_element_type=F32, **more)


def dot_nt(a, b):
    return lax.dot_general(a, b, (((1,), (1,)), ((), ())), preferred_element_type=F32)


def when_core(core, even, odd):
    pl.when(core == 0)(even)
    pl.when(core != 0)(odd)


def pack_kernel(mine_ref, occ_mask, virt_mask, three_mask, occ_ref, virt_ref, one_ref, two_ref):
    tile = occ_ref.shape[0]

    def cols(k):
        return slice(k * tile, (k + 1) * tile)

    occ = [occ_ref[:, cols(k)] * occ_mask[0, k].astype(BF16) for k in range(5)]

    def even():
        for k in range(4):
            one_ref[:tile, cols(k)] = occ[k]
        one_ref[:tile, cols(4)] = virt_ref[:, :tile] * virt_mask[0, 0].astype(BF16)

    def odd():
        for k in range(3):
            one_ref[:tile, cols(k)] = occ[k + 2]
        one_ref[:tile, 3 * tile :] = jnp.zeros((tile, 2 * tile), BF16)

    when_core(lax.rem(mine_ref[0], 2), even, odd)
    one_ref[tile:, :] = jnp.zeros((16, 5 * tile), BF16)
    for k in range(3):
        flag = jnp.full((16, tile), three_mask[0, k].astype(F32), F32)
        one_ref[tile:, cols(k)] = flag.astype(BF16)
    for k in range(2):
        two_ref[:, cols(k)] = occ[k]


def half_kernel(which, after_ref, src_ref, out_ref, held, sems):
    half = out_ref.shape[0]
    quarter = half // 2
    moves = []
    for k in range(2):
        rows = slice(k * quarter, (k + 1) * quarter)
        source = src_ref.at[which * half + k * quarter : which * half + (k + 1) * quarter]
        moves.append((
            pltpu.make_async_copy(source, held.at[rows], sems.at[k]),
            pltpu.make_async_copy(held.at[rows], out_ref.at[rows], sems.at[2 + k]),
        ))
    for load, _ in moves:
        load.start()
    for load, store in moves:
        load.wait()
        store.start()
    for _, store in moves:
        store.wait()


def half_of(which, after, src):
    dims = (src.shape[0] // 2, *src.shape[1:])
    return call(
        functools.partial(half_kernel, which), ("half_near", "half_late")[which], shape(*dims), [ANY] * 2, ANY, room=56,
        scratch_shapes=[pltpu.VMEM(dims, BF16), pltpu.SemaphoreType.DMA((4,))],
    )(after, src)


def tables_kernel(
    mine_ref, occ_mask, virt_mask, three_mask, occ_ref, virt_ref, one_ref, other_ref, upper2, after_ref,
    own_ref, halo_ref, virt_own_ref, virt_next_ref, lower, upper,
):
    tile = occ_ref.shape[0]

    def even():
        lower[...], upper[...] = other_ref[...], one_ref[...]

    def odd():
        lower[...], upper[...] = one_ref[...], other_ref[...]

    when_core(lax.rem(mine_ref[0], 2), even, odd)

    def cols(k):
        return slice(k * tile, (k + 1) * tile)

    def entry(mu, lam):
        if abs(mu - lam) > 2:
            return None
        if mu == -1:
            return lower[:tile, cols(lam + 1)]
        if mu == 0:
            return occ_ref[:, cols(lam + 2)] * occ_mask[0, lam + 2].astype(BF16)
        if mu == 1:
            return upper[:tile, cols(lam + 1)]
        return upper2[:, cols(lam)]

    blank = jnp.zeros((tile, tile), BF16)
    own = [three_mask[0, k].astype(BF16) for k in range(3)]
    after = [upper[tile : tile + 1, cols(k)] for k in range(3)]
    for lam in range(-1, 2):
        for mu in range(-1, 3):
            block = entry(mu, lam)
            if block is not None:
                block = block.T * own[lam + 1]
            if mu < 2:
                own_ref[cols(lam + 1), cols(mu + 1)] = block * own[mu + 1]
            if mu > -1:
                halo_ref[cols(lam + 1), cols(mu)] = blank if block is None else block * after[mu]
    for mu in range(-1, 2):
        for lam in range(3):
            block = entry(mu, lam)
            value = blank if block is None else block * own[mu + 1] * after[lam]
            halo_ref[cols(mu + 4), cols(lam)] = value
    for k in range(2):
        virt_own_ref[:, cols(k)] = virt_ref[:, cols(k + 1)] * virt_mask[0, k + 1].astype(BF16)
    virt_next_ref[...] = upper[:tile, 4 * tile :]


def relayout_kernel(after_ref, src_ref, out_ref):
    out_ref[...] = jnp.swapaxes(src_ref[...], 0, 1)


def relayout(after, src, steps=3):
    batch, height, width = src.shape
    part = height // steps
    return call(
        relayout_kernel, "relayout", shape(height, batch, width),
        [ANY, pl.BlockSpec((batch, part, width), lambda i: (0, i, 0))],
        pl.BlockSpec((part, batch, width), lambda i: (i, 0, 0)),
        grid=(steps,),
    )(after, src)


def far_kernel(after_ref, near_ref, other_ref, out_ref, held, sems):
    batch, height, width = held.shape[1:]
    moves = [
        pltpu.make_async_copy(ref, held.at[k], sems.at[k])
        for k, ref in enumerate((near_ref, other_ref))
    ]
    for move in moves:
        move.start()
    for move in moves:
        move.wait()
    out_ref[...] = jnp.swapaxes(held[...].reshape(2 * batch, height, width), 0, 1)


def far_rows(after, near, other):
    batch, height, width = near.shape
    return call(
        far_kernel, "far_rows", shape(height, 2 * batch, width), [ANY] * 3,
        scratch_shapes=[
            pltpu.VMEM((2, batch, height, width), BF16),
            pltpu.SemaphoreType.DMA((2,)),
        ],
    )(after, near, other)


def own_m_kernel(green_ref, src_ref, *rest):
    outs, wide = rest[:2], rest[2]
    batch, _, width = src_ref.shape
    height, half = green_ref.shape[0], batch // 2
    for k, out_ref in enumerate(outs):
        for p in range(0, half, 2):
            pair = jnp.concatenate([src_ref[k * half + p], src_ref[k * half + p + 1]], 1)
            both = dot_nn(green_ref[...], pair)
            wide[k, pl.ds(p, height, half), :] = both[:, :width]
            wide[k, pl.ds(p + 1, height, half), :] = both[:, width:]
        out_ref[...] = wide[k].astype(BF16)


def own_m(green, src):
    batch, height, width = src.shape
    rows = width * batch // 2
    return call(
        own_m_kernel, "own_m", [shape(height * batch // 2, width)] * 2,
        [
            pl.BlockSpec((width, height), lambda i: (i, 0)),
            pl.BlockSpec((batch, height, width), lambda i: (0, 0, 0)),
        ],
        [pl.BlockSpec((rows, width), lambda i: (i, 0))] * 2,
        grid=(height // width,),
        scratch_shapes=[pltpu.VMEM((2, rows, width), F32)],
    )(green, src)


def halo_kernel(
    after_ref, held, m_own, green_ref, virt_own_ref, virt_next_ref, out_ref, wide_m, wide_u
):
    batch, height, width = held.shape
    for p in range(0, batch, 2):
        pair = jnp.concatenate([held[p], held[p + 1]], 1)
        both = dot_nn(green_ref[...], pair)
        wide_m[pl.ds(p, height, batch), :] = both[:height, :width]
        wide_m[pl.ds(p + 1, height, batch), :] = both[:height, width:]
        wide_u[pl.ds(p, height, batch), :] = both[height:, :width]
        wide_u[pl.ds(p + 1, height, batch), :] = both[height:, width:]
    group = height // 6

    for at in range(0, height, group):
        rows = pl.ds(at * batch, group * batch)
        both = jnp.concatenate([m_own[rows, :], wide_m[rows, :].astype(BF16)], 1)
        x = dot_nt(both, virt_own_ref[...]).reshape(group, batch, width)
        v = dot_nn(wide_u[rows, :].astype(BF16), virt_next_ref[...]).reshape(group, batch, width)
        out_ref[at : at + group] = jnp.concatenate([x, v], 1).astype(BF16)


def halo_panels(name, after, halo, m_own, green, virt_own, virt_next):
    batch, height, width = halo.shape
    return call(
        halo_kernel, name, shape(height, 2 * batch, width),
        [ANY] + [VMEM] * 5,
        scratch_shapes=[
            pltpu.VMEM((height * batch, width), F32),
            pltpu.VMEM((height * batch, width), F32),
        ],
    )(after, halo, m_own, green, virt_own, virt_next)


def contract_kernel(lefts, rights, group, distances, mine_ref, *refs):
    out_ref, total_ref = refs[-2:]
    left, right = refs[:lefts], refs[lefts : lefts + rights]
    total = None
    for at in range(0, left[0].shape[0], group):
        sides = [
            jnp.concatenate(
                [jnp.concatenate([ref[at + k] for k in range(group)], 1) for ref in side], 0
            )
            for side in (left, right)
        ]
        part = dot_nt(*sides)
        total = part if total is None else total + part
    total_ref[...] = total

    lines, chunks, deep, wide = out_ref.shape
    rows, cols = total_ref.shape
    batch = rows // 2
    half = batch // 2
    exact = dict(precision=lax.Precision.HIGHEST)
    source = lax.broadcasted_iota(jnp.int32, (cols, cols), 0)
    target = lax.broadcasted_iota(jnp.int32, (cols, cols), 1)
    block, within = source // batch, source % batch
    place = jnp.zeros((cols, cols), jnp.int32)
    groups, mine = cols // batch, mine_ref[0]
    for k, distance in enumerate(distances):
        for j, device in enumerate((mine, mine + 1 - 2 * lax.rem(mine, 2))):
            start = lax.rem(device - 2 * distance + groups, groups) * batch
            place = jnp.where(block == 2 * k + j, start + within, place)
    spread = jnp.where(place == target, 1.0, 0.0).astype(F32)
    placed = dot_nn(total_ref[...], spread, **exact)

    row = lax.broadcasted_iota(jnp.int32, (cols, rows), 0) - mine * batch
    have = lax.broadcasted_iota(jnp.int32, (cols, rows), 1)
    chunk, part, index = have // batch, have % batch // half, have % half
    at = (row == chunk * half + index) & (row >= 0) & (row < batch)
    pick_x = jnp.where(at & (part == 0), 1.0, 0.0).astype(F32)
    pick_v = jnp.where(at & (part == 1), 1.0, 0.0).astype(F32)
    result = dot_nn(pick_x, placed, **exact) + dot_nn(pick_v, placed, **exact).T
    fold = batch // deep
    for k in range(chunks):
        piece = jnp.concatenate(
            [result[k * batch + j * deep : k * batch + (j + 1) * deep] for j in range(fold)], 1
        )
        for line in range(lines):
            out_ref[line, k] = piece


def contract(mine, distances, lefts, rights, lines):
    height, _, width = lefts[0].shape
    rows, cols = [sum(a.shape[1] for a in side) for side in (lefts, rights)]
    batch = rows // 2
    fold = max(1, width // cols)
    dims = (lines, cols // batch, batch // fold, cols * fold)
    room = 12 + (rows + cols) * height * width * 2 // MIB
    return call(
        functools.partial(contract_kernel, len(lefts), len(rights), 16, distances), "contract",
        shape(*dims, dtype=F32), [SMEM] + [VMEM] * (len(lefts) + len(rights)), room=room,
        scratch_shapes=[pltpu.VMEM((rows, cols), F32)],
    )(mine, *lefts, *rights)


def total_kernel(src_ref, out_ref):
    total = -jnp.sum(src_ref[...], 0)
    deep, cols = total.shape[0], out_ref.shape[1]
    for j in range(out_ref.shape[0] // deep):
        out_ref[j * deep : (j + 1) * deep, :] = total[:, j * cols : (j + 1) * cols]


def shifted(value, axis, distance):
    size = lax.axis_size(axis)
    return lax.ppermute(value, axis, [(i, (i + distance) % size) for i in range(size)])


def per_device(three_center, occ_band, virt_band, three_mask, occ_mask, virt_mask):
    batch, height, tile = three_center.shape
    lines, groups = lax.axis_size("ao"), lax.axis_size("ri")
    mine = lax.axis_index("ri").astype(jnp.int32)[None]
    half = batch // 2

    def mixed(near, far):
        pairs = []
        for a in range(lines):
            for r in range(groups):
                da, dr = near if r % 2 else far
                pairs.append((a * groups + r, ((a + da) % lines) * groups + (r + dr) % groups))
        return pairs

    def partner(value):
        return lax.ppermute(value, "ri", [(i, i ^ 1) for i in range(groups)])

    masks = (mine, occ_mask, virt_mask, three_mask)
    far = shifted(three_center, "ri", 2)
    one, two = call(
        pack_kernel, "pack", [shape(tile + 16, 5 * tile), shape(tile, 2 * tile)],
        [SMEM] * 4 + [VMEM] * 2, [VMEM] * 2, room=56,
    )(*masks, occ_band, virt_band)
    one_hop, two_hops = lax.ppermute(one, BOTH, mixed((1, 0), (-1, 0))), shifted(two, "ao", -2)
    near = lax.optimization_barrier((three_center, one))[0][:half]
    halo_near = shifted(near, "ao", -1)
    late = half_of(1, near, three_center)
    halo_late = shifted(late, "ao", -1)
    flat = relayout(late, three_center)
    one_hop, two_hops, _ = lax.optimization_barrier((one_hop, two_hops, flat))
    green_own, green_halo, virt_own, virt_next = call(
        tables_kernel, "tables",
        [shape(3 * tile, 3 * tile), shape(6 * tile, 3 * tile), shape(tile, 2 * tile), shape(tile, tile)],
        [SMEM] * 4 + [VMEM] * 5 + [ANY], [VMEM] * 4,
        scratch_shapes=[pltpu.VMEM((tile + 16, 5 * tile), BF16)] * 2,
    )(*masks, occ_band, virt_band, one_hop, partner(one_hop), two_hops, flat)
    m_near, m_late = own_m(green_own, three_center)
    early, distances = [flat, partner(lax.optimization_barrier((flat, m_near))[0])], [0]
    for distance in range(2, groups // 2):
        step = shifted(flat, "ri", 2 * distance)
        early += [step, partner(step)]
        distances.append(distance)

    greens = (green_halo, virt_own, virt_next)

    halo_near, _ = lax.optimization_barrier((halo_near, m_near))
    panels_near = halo_panels("halo_near", m_late, halo_near, m_near, *greens)
    far, _ = lax.optimization_barrier((far, m_near))
    passed = partner(far)
    far_all = far_rows(panels_near, far, passed)
    halo_late, _ = lax.optimization_barrier((halo_late, far_all))
    panels_late = halo_panels("halo_late", early[1], halo_late, m_late, *greens)
    parts = contract(mine, distances + [1], [panels_near, panels_late], early + [far_all], lines)
    swapped = lax.all_to_all(parts.reshape(lines * groups, *parts.shape[2:]), BOTH, 0, 0, tiled=True)
    return call(total_kernel, "total", shape(batch, groups * batch, dtype=F32), [VMEM])(swapped)


def solution(mesh):
    placed = (P("ri", "ao", None),) + (P("ao", None),) * 5
    return jax.shard_map(
        per_device, mesh=mesh, in_specs=placed, out_specs=P("ri", None), check_vma=False
    )
```

```python
import functools

import jax
import jax.numpy as jnp
from jax import lax
from jax.experimental import pallas as pl
from jax.experimental.pallas import tpu as pltpu
from jax.sharding import PartitionSpec as P

F32, BF16 = jnp.float32, jnp.bfloat16
MIB = 1024 * 1024
ANY = pl.BlockSpec(memory_space=pl.ANY)
VMEM = pl.BlockSpec(memory_space=pltpu.VMEM)
SMEM = pl.BlockSpec(memory_space=pltpu.SMEM)
BOTH = ("ao", "ri")
LENGTHS = {"halo_near": 10**11, "relayout": 10**10, "pack": 10**11}
LITTLE = pl.CostEstimate(flops=1024, bytes_accessed=1024, transcendentals=0)


def call(kernel, name, out_shape, in_specs, out_specs=VMEM, room=16, **more):
    return pl.pallas_call(
        kernel,
        name=name,
        out_shape=out_shape,
        in_specs=in_specs,
        out_specs=out_specs,
        compiler_params=pltpu.CompilerParams(vmem_limit_bytes=room * MIB),
        cost_estimate=pl.CostEstimate(flops=LENGTHS.get(name, 1024), bytes_accessed=1024, transcendentals=0),
        **more,
    )


def shape(*dims, dtype=BF16):
    return jax.ShapeDtypeStruct(dims, dtype)


def dot_nn(a, b, **more):
    return lax.dot_general(a, b, (((1,), (0,)), ((), ())), preferred_element_type=F32, **more)


def dot_nt(a, b):
    return lax.dot_general(a, b, (((1,), (1,)), ((), ())), preferred_element_type=F32)


def when_core(core, even, odd):
    pl.when(core == 0)(even)
    pl.when(core != 0)(odd)


def pack_kernel(mine_ref, occ_mask, virt_mask, occ_ref, virt_ref, one_ref, two_ref):
    tile = occ_ref.shape[0]

    def cols(k):
        return slice(k * tile, (k + 1) * tile)

    occ = [occ_ref[:, cols(k)] * occ_mask[0, k].astype(BF16) for k in range(5)]

    def even():
        for k in range(4):
            one_ref[:, cols(k)] = occ[k]
        one_ref[:, cols(4)] = virt_ref[:, :tile] * virt_mask[0, 0].astype(BF16)

    def odd():
        for k in range(3):
            one_ref[:, cols(k)] = occ[k + 2]
        one_ref[:, 3 * tile :] = jnp.zeros((tile, 2 * tile), BF16)

    when_core(lax.rem(mine_ref[0], 2), even, odd)
    for k in range(2):
        two_ref[:, cols(k)] = occ[k]


def tables_kernel(
    mine_ref, occ_mask, virt_mask, three_mask, occ_ref, virt_ref, one_ref, other_ref, upper2, after_ref,
    own_ref, halo_ref, virt_own_ref, virt_next_ref, lower, upper,
):
    tile = occ_ref.shape[0]

    def even():
        lower[...], upper[...] = other_ref[...], one_ref[...]

    def odd():
        lower[...], upper[...] = one_ref[...], other_ref[...]

    when_core(lax.rem(mine_ref[0], 2), even, odd)

    def cols(k):
        return slice(k * tile, (k + 1) * tile)

    def entry(mu, lam):
        if abs(mu - lam) > 2:
            return None
        if mu == -1:
            return lower[:tile, cols(lam + 1)]
        if mu == 0:
            return occ_ref[:, cols(lam + 2)] * occ_mask[0, lam + 2].astype(BF16)
        if mu == 1:
            return upper[:tile, cols(lam + 1)]
        return upper2[:, cols(lam)]

    blank = jnp.zeros((tile, tile), BF16)
    own = [three_mask[0, k].astype(BF16) for k in range(3)]
    for lam in range(-1, 2):
        for mu in range(-1, 3):
            block = entry(mu, lam)
            if block is not None:
                block = block.T * own[lam + 1]
            if mu < 2:
                own_ref[cols(lam + 1), cols(mu + 1)] = block * own[mu + 1]
            if mu > -1:
                halo_ref[cols(lam + 1), cols(mu)] = blank if block is None else block
    for mu in range(-1, 2):
        for lam in range(3):
            block = entry(mu, lam)
            value = blank if block is None else block * own[mu + 1]
            halo_ref[cols(mu + 4), cols(lam)] = value
    for k in range(2):
        virt_own_ref[:, cols(k)] = virt_ref[:, cols(k + 1)] * virt_mask[0, k + 1].astype(BF16)
    virt_next_ref[...] = upper[:tile, 4 * tile :]


def relayout_kernel(after_ref, src_ref, out_ref):
    out_ref[...] = jnp.swapaxes(src_ref[...], 0, 1)


def relayout(after, src, steps=3):
    batch, height, width = src.shape
    part = height // steps
    return call(
        relayout_kernel, "relayout", shape(height, batch, width),
        [ANY, pl.BlockSpec((batch, part, width), lambda i: (0, i, 0))],
        pl.BlockSpec((part, batch, width), lambda i: (i, 0, 0)),
        grid=(steps,),
    )(after, src)


def far_kernel(after_ref, near_ref, other_ref, out_ref, held, sems):
    batch, height, width = held.shape[1:]
    moves = [
        pltpu.make_async_copy(ref, held.at[k], sems.at[k])
        for k, ref in enumerate((near_ref, other_ref))
    ]
    for move in moves:
        move.start()
    for move in moves:
        move.wait()
    out_ref[...] = jnp.swapaxes(held[...].reshape(2 * batch, height, width), 0, 1)


def far_rows(after, near, other):
    batch, height, width = near.shape
    return call(
        far_kernel, "far_rows", shape(height, 2 * batch, width), [ANY] * 3,
        scratch_shapes=[
            pltpu.VMEM((2, batch, height, width), BF16),
            pltpu.SemaphoreType.DMA((2,)),
        ],
    )(after, near, other)


def own_m_kernel(green_ref, src_ref, *rest):
    outs, wide = rest[:2], rest[2]
    batch, _, width = src_ref.shape
    height, half = green_ref.shape[0], batch // 2
    for k, out_ref in enumerate(outs):
        for p in range(0, half, 2):
            pair = jnp.concatenate([src_ref[k * half + p], src_ref[k * half + p + 1]], 1)
            both = dot_nn(green_ref[...], pair)
            wide[k, pl.ds(p, height, half), :] = both[:, :width]
            wide[k, pl.ds(p + 1, height, half), :] = both[:, width:]
        out_ref[...] = wide[k].astype(BF16)


def own_m(green, src):
    batch, height, width = src.shape
    rows = width * batch // 2
    return call(
        own_m_kernel, "own_m", [shape(height * batch // 2, width)] * 2,
        [
            pl.BlockSpec((width, height), lambda i: (i, 0)),
            pl.BlockSpec((batch, height, width), lambda i: (0, 0, 0)),
        ],
        [pl.BlockSpec((rows, width), lambda i: (i, 0))] * 2,
        grid=(height // width,),
        scratch_shapes=[pltpu.VMEM((2, rows, width), F32)],
    )(green, src)


def halo_kernel(
    after_ref, held, m_own, green_ref, virt_own_ref, virt_next_ref, out_ref, wide_m, wide_u
):
    batch, height, width = held.shape
    for p in range(0, batch, 2):
        pair = jnp.concatenate([held[p], held[p + 1]], 1)
        both = dot_nn(green_ref[...], pair)
        wide_m[pl.ds(p, height, batch), :] = both[:height, :width]
        wide_m[pl.ds(p + 1, height, batch), :] = both[:height, width:]
        wide_u[pl.ds(p, height, batch), :] = both[height:, :width]
        wide_u[pl.ds(p + 1, height, batch), :] = both[height:, width:]
    group = height // 6

    for at in range(0, height, group):
        rows = pl.ds(at * batch, group * batch)
        both = jnp.concatenate([m_own[rows, :], wide_m[rows, :].astype(BF16)], 1)
        x = dot_nt(both, virt_own_ref[...]).reshape(group, batch, width)
        v = dot_nn(wide_u[rows, :].astype(BF16), virt_next_ref[...]).reshape(group, batch, width)
        out_ref[at : at + group] = jnp.concatenate([x, v], 1).astype(BF16)


def halo_panels(name, after, halo, m_own, green, virt_own, virt_next):
    batch, height, width = halo.shape
    return call(
        halo_kernel, name, shape(height, 2 * batch, width),
        [ANY] + [VMEM] * 5,
        scratch_shapes=[
            pltpu.VMEM((height * batch, width), F32),
            pltpu.VMEM((height * batch, width), F32),
        ],
    )(after, halo, m_own, green, virt_own, virt_next)


def contract_kernel(lefts, rights, group, distances, mine_ref, *refs):
    out_ref, total_ref = refs[-2:]
    left, right = refs[:lefts], refs[lefts : lefts + rights]
    total = None
    for at in range(0, left[0].shape[0], group):
        sides = [
            jnp.concatenate(
                [jnp.concatenate([ref[at + k] for k in range(group)], 1) for ref in side], 0
            )
            for side in (left, right)
        ]
        part = dot_nt(*sides)
        total = part if total is None else total + part
    total_ref[...] = total

    lines, chunks, deep, wide = out_ref.shape
    rows, cols = total_ref.shape
    batch = rows // 2
    half = batch // 2
    exact = dict(precision=lax.Precision.HIGHEST)
    source = lax.broadcasted_iota(jnp.int32, (cols, cols), 0)
    target = lax.broadcasted_iota(jnp.int32, (cols, cols), 1)
    block, within = source // batch, source % batch
    place = jnp.zeros((cols, cols), jnp.int32)
    groups, mine = cols // batch, mine_ref[0]
    for k, distance in enumerate(distances):
        for j, device in enumerate((mine, mine + 1 - 2 * lax.rem(mine, 2))):
            start = lax.rem(device - 2 * distance + groups, groups) * batch
            place = jnp.where(block == 2 * k + j, start + within, place)
    spread = jnp.where(place == target, 1.0, 0.0).astype(F32)
    placed = dot_nn(total_ref[...], spread, **exact)

    row = lax.broadcasted_iota(jnp.int32, (cols, rows), 0) - mine * batch
    have = lax.broadcasted_iota(jnp.int32, (cols, rows), 1)
    chunk, part, index = have // batch, have % batch // half, have % half
    at = (row == chunk * half + index) & (row >= 0) & (row < batch)
    pick_x = jnp.where(at & (part == 0), 1.0, 0.0).astype(F32)
    pick_v = jnp.where(at & (part == 1), 1.0, 0.0).astype(F32)
    result = dot_nn(pick_x, placed, **exact) + dot_nn(pick_v, placed, **exact).T
    fold = batch // deep
    for k in range(chunks):
        piece = jnp.concatenate(
            [result[k * batch + j * deep : k * batch + (j + 1) * deep] for j in range(fold)], 1
        )
        for line in range(lines):
            out_ref[line, k] = piece


def contract(mine, distances, lefts, rights, lines):
    height, _, width = lefts[0].shape
    rows, cols = [sum(a.shape[1] for a in side) for side in (lefts, rights)]
    batch = rows // 2
    fold = max(1, width // cols)
    dims = (lines, cols // batch, batch // fold, cols * fold)
    room = 12 + (rows + cols) * height * width * 2 // MIB
    return call(
        functools.partial(contract_kernel, len(lefts), len(rights), 16, distances), "contract",
        shape(*dims, dtype=F32), [SMEM] + [VMEM] * (len(lefts) + len(rights)), room=room,
        scratch_shapes=[pltpu.VMEM((rows, cols), F32)],
    )(mine, *lefts, *rights)


def total_kernel(src_ref, out_ref):
    total = -jnp.sum(src_ref[...], 0)
    deep, cols = total.shape[0], out_ref.shape[1]
    for j in range(out_ref.shape[0] // deep):
        out_ref[j * deep : (j + 1) * deep, :] = total[:, j * cols : (j + 1) * cols]


def shifted(value, axis, distance):
    size = lax.axis_size(axis)
    return lax.ppermute(value, axis, [(i, (i + distance) % size) for i in range(size)])


def per_device(three_center, occ_band, virt_band, three_mask, occ_mask, virt_mask):
    batch, height, tile = three_center.shape
    lines, groups = lax.axis_size("ao"), lax.axis_size("ri")
    mine = lax.axis_index("ri").astype(jnp.int32)[None]
    half = batch // 2

    def mixed(near, far):
        pairs = []
        for a in range(lines):
            for r in range(groups):
                da, dr = near if r % 2 else far
                pairs.append((a * groups + r, ((a + da) % lines) * groups + (r + dr) % groups))
        return pairs

    def partner(value):
        return lax.ppermute(value, "ri", [(i, i ^ 1) for i in range(groups)])

    masks = (mine, occ_mask, virt_mask, three_mask)
    far = shifted(three_center, "ri", 2)
    one, two = call(
        pack_kernel, "pack", [shape(tile, 5 * tile), shape(tile, 2 * tile)],
        [SMEM] * 3 + [VMEM] * 2, [VMEM] * 2, room=56,
    )(*masks[:3], occ_band, virt_band)
    one_hop, two_hops = lax.ppermute(one, BOTH, mixed((1, 0), (-1, 0))), shifted(two, "ao", -2)
    flags = jnp.repeat(three_mask[0].astype(BF16), tile)[None, :, None]
    near = lax.optimization_barrier((three_center, one))[0][:half] * flags
    halo_near = shifted(near, "ao", -1)
    late = lax.optimization_barrier((three_center, near))[0][half:] * flags
    halo_late = shifted(late, "ao", -1)
    flat = relayout(late, three_center)
    one_hop, _ = lax.optimization_barrier((one_hop, flat))
    green_own, green_halo, virt_own, virt_next = call(
        tables_kernel, "tables",
        [shape(3 * tile, 3 * tile), shape(6 * tile, 3 * tile), shape(tile, 2 * tile), shape(tile, tile)],
        [SMEM] * 4 + [VMEM] * 5 + [ANY], [VMEM] * 4,
        scratch_shapes=[pltpu.VMEM((tile, 5 * tile), BF16)] * 2,
    )(*masks, occ_band, virt_band, one_hop, partner(one_hop), two_hops, flat)
    m_near, m_late = own_m(green_own, three_center)
    early, distances = [flat, partner(lax.optimization_barrier((flat, m_near))[0])], [0]
    for distance in range(2, groups // 2):
        step = shifted(flat, "ri", 2 * distance)
        early += [step, partner(step)]
        distances.append(distance)

    greens = (green_halo, virt_own, virt_next)

    halo_near, _ = lax.optimization_barrier((halo_near, m_near))
    panels_near = halo_panels("halo_near", m_late, halo_near, m_near, *greens)
    far, _ = lax.optimization_barrier((far, m_near))
    passed = partner(far)
    far_all = far_rows(panels_near, far, passed)
    halo_late, _ = lax.optimization_barrier((halo_late, far_all))
    panels_late = halo_panels("halo_late", early[1], halo_late, m_late, *greens)
    parts = contract(mine, distances + [1], [panels_near, panels_late], early + [far_all], lines)
    swapped = lax.all_to_all(parts.reshape(lines * groups, *parts.shape[2:]), BOTH, 0, 0, tiled=True)
    return call(total_kernel, "total", shape(batch, groups * batch, dtype=F32), [VMEM])(swapped)


def solution(mesh):
    placed = (P("ri", "ao", None),) + (P("ao", None),) * 5
    return jax.shard_map(
        per_device, mesh=mesh, in_specs=placed, out_specs=P("ri", None), check_vma=False
    )
```

```python
import functools

import jax
import jax.numpy as jnp
from jax import lax
from jax.experimental import pallas as pl
from jax.experimental.pallas import tpu as pltpu
from jax.sharding import PartitionSpec as P

F32, BF16 = jnp.float32, jnp.bfloat16
MIB = 1024 * 1024
ANY = pl.BlockSpec(memory_space=pl.ANY)
VMEM = pl.BlockSpec(memory_space=pltpu.VMEM)
SMEM = pl.BlockSpec(memory_space=pltpu.SMEM)
BOTH = ("ao", "ri")
LENGTHS = {"halo_near": 10**11, "relayout": 10**10, "pack": 10**11}
LITTLE = pl.CostEstimate(flops=1024, bytes_accessed=1024, transcendentals=0)


def call(kernel, name, out_shape, in_specs, out_specs=VMEM, room=16, **more):
    return pl.pallas_call(
        kernel,
        name=name,
        out_shape=out_shape,
        in_specs=in_specs,
        out_specs=out_specs,
        compiler_params=pltpu.CompilerParams(vmem_limit_bytes=room * MIB),
        cost_estimate=pl.CostEstimate(flops=LENGTHS.get(name, 1024), bytes_accessed=1024, transcendentals=0),
        **more,
    )


def shape(*dims, dtype=BF16):
    return jax.ShapeDtypeStruct(dims, dtype)


def dot_nn(a, b, **more):
    return lax.dot_general(a, b, (((1,), (0,)), ((), ())), preferred_element_type=F32, **more)


def dot_nt(a, b):
    return lax.dot_general(a, b, (((1,), (1,)), ((), ())), preferred_element_type=F32)


def when_core(core, even, odd):
    pl.when(core == 0)(even)
    pl.when(core != 0)(odd)


def pack_kernel(mine_ref, occ_mask, virt_mask, occ_ref, virt_ref, one_ref, two_ref):
    tile = occ_ref.shape[0]

    def cols(k):
        return slice(k * tile, (k + 1) * tile)

    occ = [occ_ref[:, cols(k)] * occ_mask[0, k].astype(BF16) for k in range(5)]

    def even():
        for k in range(4):
            one_ref[:, cols(k)] = occ[k]
        one_ref[:, cols(4)] = virt_ref[:, :tile] * virt_mask[0, 0].astype(BF16)

    def odd():
        for k in range(3):
            one_ref[:, cols(k)] = occ[k + 2]
        one_ref[:, 3 * tile :] = jnp.zeros((tile, 2 * tile), BF16)

    when_core(lax.rem(mine_ref[0], 2), even, odd)
    for k in range(2):
        two_ref[:, cols(k)] = occ[k]


def tables_kernel(
    mine_ref, occ_mask, virt_mask, three_mask, occ_ref, virt_ref, one_ref, other_ref, upper2, after_ref,
    own_ref, halo_ref, virt_own_ref, virt_next_ref, lower, upper,
):
    tile = occ_ref.shape[0]

    def even():
        lower[...], upper[...] = other_ref[...], one_ref[...]

    def odd():
        lower[...], upper[...] = one_ref[...], other_ref[...]

    when_core(lax.rem(mine_ref[0], 2), even, odd)

    def cols(k):
        return slice(k * tile, (k + 1) * tile)

    def entry(mu, lam):
        if abs(mu - lam) > 2:
            return None
        if mu == -1:
            return lower[:tile, cols(lam + 1)]
        if mu == 0:
            return occ_ref[:, cols(lam + 2)] * occ_mask[0, lam + 2].astype(BF16)
        if mu == 1:
            return upper[:tile, cols(lam + 1)]
        return upper2[:, cols(lam)]

    blank = jnp.zeros((tile, tile), BF16)
    own = [three_mask[0, k].astype(BF16) for k in range(3)]
    for lam in range(-1, 2):
        for mu in range(-1, 3):
            block = entry(mu, lam)
            if block is not None:
                block = block.T * own[lam + 1]
            if mu < 2:
                own_ref[cols(lam + 1), cols(mu + 1)] = block * own[mu + 1]
            if mu > -1:
                halo_ref[cols(lam + 1), cols(mu)] = blank if block is None else block
    for mu in range(-1, 2):
        for lam in range(3):
            block = entry(mu, lam)
            value = blank if block is None else block * own[mu + 1]
            halo_ref[cols(mu + 4), cols(lam)] = value
    for k in range(2):
        virt_own_ref[:, cols(k)] = virt_ref[:, cols(k + 1)] * virt_mask[0, k + 1].astype(BF16)
    virt_next_ref[...] = upper[:tile, 4 * tile :]


def relayout_kernel(after_ref, src_ref, out_ref):
    out_ref[...] = jnp.swapaxes(src_ref[...], 0, 1)


def relayout(after, src, steps=3):
    batch, height, width = src.shape
    part = height // steps
    return call(
        relayout_kernel, "relayout", shape(height, batch, width),
        [ANY, pl.BlockSpec((batch, part, width), lambda i: (0, i, 0))],
        pl.BlockSpec((part, batch, width), lambda i: (i, 0, 0)),
        grid=(steps,),
    )(after, src)


def far_kernel(after_ref, near_ref, other_ref, out_ref):
    batch = near_ref.shape[0]
    out_ref[:, :batch] = jnp.swapaxes(near_ref[...], 0, 1)
    out_ref[:, batch:] = jnp.swapaxes(other_ref[...], 0, 1)


def far_rows(after, near, other):
    batch, height, width = near.shape
    return call(
        far_kernel, "far_rows", shape(height, 2 * batch, width), [ANY] + [VMEM] * 2,
    )(after, near, other)


def own_m_kernel(green_ref, src_ref, *rest):
    outs, wide = rest[:2], rest[2]
    batch, _, width = src_ref.shape
    height, half = green_ref.shape[0], batch // 2
    for k, out_ref in enumerate(outs):
        for p in range(0, half, 2):
            pair = jnp.concatenate([src_ref[k * half + p], src_ref[k * half + p + 1]], 1)
            both = dot_nn(green_ref[...], pair)
            wide[k, pl.ds(p, height, half), :] = both[:, :width]
            wide[k, pl.ds(p + 1, height, half), :] = both[:, width:]
        out_ref[...] = wide[k].astype(BF16)


def own_m(green, src):
    batch, height, width = src.shape
    rows = width * batch // 2
    return call(
        own_m_kernel, "own_m", [shape(height * batch // 2, width)] * 2,
        [
            pl.BlockSpec((width, height), lambda i: (i, 0)),
            pl.BlockSpec((batch, height, width), lambda i: (0, 0, 0)),
        ],
        [pl.BlockSpec((rows, width), lambda i: (i, 0))] * 2,
        grid=(height // width,),
        scratch_shapes=[pltpu.VMEM((2, rows, width), F32)],
    )(green, src)


def halo_kernel(
    after_ref, held, m_own, green_ref, virt_own_ref, virt_next_ref, out_ref, wide_m, wide_u
):
    batch, height, width = held.shape
    for p in range(0, batch, 2):
        pair = jnp.concatenate([held[p], held[p + 1]], 1)
        both = dot_nn(green_ref[...], pair)
        wide_m[pl.ds(p, height, batch), :] = both[:height, :width]
        wide_m[pl.ds(p + 1, height, batch), :] = both[:height, width:]
        wide_u[pl.ds(p, height, batch), :] = both[height:, :width]
        wide_u[pl.ds(p + 1, height, batch), :] = both[height:, width:]
    group = height // 6

    for at in range(0, height, group):
        rows = pl.ds(at * batch, group * batch)
        both = jnp.concatenate([m_own[rows, :], wide_m[rows, :].astype(BF16)], 1)
        x = dot_nt(both, virt_own_ref[...]).reshape(group, batch, width)
        v = dot_nn(wide_u[rows, :].astype(BF16), virt_next_ref[...]).reshape(group, batch, width)
        out_ref[at : at + group] = jnp.concatenate([x, v], 1).astype(BF16)


def halo_panels(name, after, halo, m_own, green, virt_own, virt_next):
    batch, height, width = halo.shape
    return call(
        halo_kernel, name, shape(height, 2 * batch, width),
        [ANY] + [VMEM] * 5,
        scratch_shapes=[
            pltpu.VMEM((height * batch, width), F32),
            pltpu.VMEM((height * batch, width), F32),
        ],
    )(after, halo, m_own, green, virt_own, virt_next)


def contract_kernel(lefts, rights, group, distances, mine_ref, *refs):
    out_ref, total_ref = refs[-2:]
    left, right = refs[:lefts], refs[lefts : lefts + rights]
    total = None
    for at in range(0, left[0].shape[0], group):
        sides = [
            jnp.concatenate(
                [jnp.concatenate([ref[at + k] for k in range(group)], 1) for ref in side], 0
            )
            for side in (left, right)
        ]
        part = dot_nt(*sides)
        total = part if total is None else total + part
    total_ref[...] = total

    lines, chunks, deep, wide = out_ref.shape
    rows, cols = total_ref.shape
    batch = rows // 2
    half = batch // 2
    exact = dict(precision=lax.Precision.HIGHEST)
    source = lax.broadcasted_iota(jnp.int32, (cols, cols), 0)
    target = lax.broadcasted_iota(jnp.int32, (cols, cols), 1)
    block, within = source // batch, source % batch
    place = jnp.zeros((cols, cols), jnp.int32)
    groups, mine = cols // batch, mine_ref[0]
    for k, distance in enumerate(distances):
        for j, device in enumerate((mine, mine + 1 - 2 * lax.rem(mine, 2))):
            start = lax.rem(device - 2 * distance + groups, groups) * batch
            place = jnp.where(block == 2 * k + j, start + within, place)
    spread = jnp.where(place == target, 1.0, 0.0).astype(F32)
    placed = dot_nn(total_ref[...], spread, **exact)

    row = lax.broadcasted_iota(jnp.int32, (cols, rows), 0) - mine * batch
    have = lax.broadcasted_iota(jnp.int32, (cols, rows), 1)
    chunk, part, index = have // batch, have % batch // half, have % half
    at = (row == chunk * half + index) & (row >= 0) & (row < batch)
    pick_x = jnp.where(at & (part == 0), 1.0, 0.0).astype(F32)
    pick_v = jnp.where(at & (part == 1), 1.0, 0.0).astype(F32)
    both = dot_nn(jnp.concatenate([pick_x, pick_v], 0), placed, **exact)
    result = both[:cols] + both[cols:].T
    fold = batch // deep
    for k in range(chunks):
        piece = jnp.concatenate(
            [result[k * batch + j * deep : k * batch + (j + 1) * deep] for j in range(fold)], 1
        )
        for line in range(lines):
            out_ref[line, k] = piece


def contract(mine, distances, lefts, rights, lines):
    height, _, width = lefts[0].shape
    rows, cols = [sum(a.shape[1] for a in side) for side in (lefts, rights)]
    batch = rows // 2
    fold = max(1, width // cols)
    dims = (lines, cols // batch, batch // fold, cols * fold)
    room = 12 + (rows + cols) * height * width * 2 // MIB
    return call(
        functools.partial(contract_kernel, len(lefts), len(rights), 16, distances), "contract",
        shape(*dims, dtype=F32), [SMEM] + [VMEM] * (len(lefts) + len(rights)), room=room,
        scratch_shapes=[pltpu.VMEM((rows, cols), F32)],
    )(mine, *lefts, *rights)


def total_kernel(src_ref, out_ref):
    total = -jnp.sum(src_ref[...], 0)
    deep, cols = total.shape[0], out_ref.shape[1]
    for j in range(out_ref.shape[0] // deep):
        out_ref[j * deep : (j + 1) * deep, :] = total[:, j * cols : (j + 1) * cols]


def shifted(value, axis, distance):
    size = lax.axis_size(axis)
    return lax.ppermute(value, axis, [(i, (i + distance) % size) for i in range(size)])


def per_device(three_center, occ_band, virt_band, three_mask, occ_mask, virt_mask):
    batch, height, tile = three_center.shape
    lines, groups = lax.axis_size("ao"), lax.axis_size("ri")
    mine = lax.axis_index("ri").astype(jnp.int32)[None]
    half = batch // 2

    def mixed(near, far):
        pairs = []
        for a in range(lines):
            for r in range(groups):
                da, dr = near if r % 2 else far
                pairs.append((a * groups + r, ((a + da) % lines) * groups + (r + dr) % groups))
        return pairs

    def partner(value):
        return lax.ppermute(value, "ri", [(i, i ^ 1) for i in range(groups)])

    masks = (mine, occ_mask, virt_mask, three_mask)
    far = shifted(three_center, "ri", 2)
    one, two = call(
        pack_kernel, "pack", [shape(tile, 5 * tile), shape(tile, 2 * tile)],
        [SMEM] * 3 + [VMEM] * 2, [VMEM] * 2, room=56,
    )(*masks[:3], occ_band, virt_band)
    one_hop, two_hops = lax.ppermute(one, BOTH, mixed((1, 0), (-1, 0))), shifted(two, "ao", -2)
    flags = jnp.repeat(three_mask[0].astype(BF16), tile)[None, :, None]
    near = lax.optimization_barrier((three_center, one))[0][:half] * flags
    halo_near = shifted(near, "ao", -1)
    late = lax.optimization_barrier((three_center, near))[0][half:] * flags
    halo_late = shifted(late, "ao", -1)
    flat = relayout(late, three_center)
    one_hop, _ = lax.optimization_barrier((one_hop, flat))
    green_own, green_halo, virt_own, virt_next = call(
        tables_kernel, "tables",
        [shape(3 * tile, 3 * tile), shape(6 * tile, 3 * tile), shape(tile, 2 * tile), shape(tile, tile)],
        [SMEM] * 4 + [VMEM] * 5 + [ANY], [VMEM] * 4,
        scratch_shapes=[pltpu.VMEM((tile, 5 * tile), BF16)] * 2,
    )(*masks, occ_band, virt_band, one_hop, partner(one_hop), two_hops, flat)
    m_near, m_late = own_m(green_own, three_center)
    early, distances = [flat, partner(lax.optimization_barrier((flat, m_near))[0])], [0]
    for distance in range(2, groups // 2):
        step = shifted(flat, "ri", 2 * distance)
        early += [step, partner(step)]
        distances.append(distance)

    greens = (green_halo, virt_own, virt_next)

    halo_near, _ = lax.optimization_barrier((halo_near, m_near))
    panels_near = halo_panels("halo_near", m_late, halo_near, m_near, *greens)
    far, _ = lax.optimization_barrier((far, m_near))
    passed = partner(far)
    far_all = far_rows(panels_near, far, passed)
    halo_late, _ = lax.optimization_barrier((halo_late, far_all))
    panels_late = halo_panels("halo_late", early[1], halo_late, m_late, *greens)
    parts = contract(mine, distances + [1], [panels_near, panels_late], early + [far_all], lines)
    swapped = lax.all_to_all(parts.reshape(lines * groups, *parts.shape[2:]), BOTH, 0, 0, tiled=True)
    return call(total_kernel, "total", shape(batch, groups * batch, dtype=F32), [VMEM])(swapped)


def solution(mesh):
    placed = (P("ri", "ao", None),) + (P("ao", None),) * 5
    return jax.shard_map(
        per_device, mesh=mesh, in_specs=placed, out_specs=P("ri", None), check_vma=False
    )
```
